256 devices in a mesh: users: 64 (over z, x, core), camp: 4 (over y).
Axes of the slice: x: 4, y: 4, z: 8, core: 2. Of those that a mesh axis runs over, the one named last changes fastest.
Arguments:
- user_emb: bfloat16 [524288, 256], P('users'), may hold values from -6 to 6
- camp_emb: bfloat16 [16384, 256], P(('camp', 'users')), may hold values from -0.375 to 0.375
- block_ids: int32 [4, 16384], P('camp', 'users'), may hold values from 0 to 2047, as said below
- block_count: int32 [4, 64], P('camp', 'users'), may hold values from 1 to 256, as said below
- capacity: int32 [16384], P('camp'), may hold values from 4096 to 21845
- user_limit: int32 [524288], P('users'), may hold values from 128 to 682
Outputs:
- duals: float32 [16384], P('camp')
- user_duals: float32 [524288], P('users')
- load_ratio: float32 [16384], P('camp')
- user_value: float32 [524288], P('users')
The draws below stay inside these ranges and needn't reach their ends.
Inputs may be any that keep to these rules, and one draw needn't show every extreme that they name: `block_ids`: within one device's 256 entries all ids differ. `block_count`: some device has all 256 entries eligible.
All inputs are finite; a program needn't handle non-finite values.
Results may differ from the reference program's by a relative error of at most 0.0005.
Values may be sent and summed in bfloat16 or wider, within the bound.
No kernel may reach another device: no remote copies, remote signals or barrier semaphores. Data moves between devices by JAX's collectives and lax.ppermute only.
A program may use at most 64 MiB of HBM per device.

```python
import jax
import jax.numpy as jnp
from jax import lax

E = 256
BLOCK = 128
U_DEV = 8192
C_GROUP = 4096
SLOTS = 256
ITERS = 3
UBLOCKS = 64
CBLOCKS = 32
USERS = 524288
CAMPAIGNS = 16384
N_USERS = 64
N_CAMP = 4


def draw_block_ids(key, part):
    key = jax.random.fold_in(key, 11)
    keys = jax.random.split(key, N_CAMP * N_USERS)
    total = U_DEV // BLOCK * (C_GROUP // BLOCK)
    picks = jax.vmap(lambda k: jax.random.permutation(k, total)[:SLOTS])(keys)
    return picks.reshape(N_CAMP, N_USERS * SLOTS).astype(jnp.int32)


def draw_block_count(key, part):
    key = jax.random.fold_in(key, 23)
    first, second = jax.random.split(key)
    counts = jax.random.randint(first, (N_CAMP * N_USERS,), max(SLOTS // 3, 1), SLOTS + 1)
    where = jax.random.randint(second, (), 0, N_CAMP * N_USERS)
    counts = counts.at[where].set(SLOTS)
    return counts.reshape(N_CAMP, N_USERS).astype(jnp.int32)


def plant(array, rng, least, largest):
    dims = array.shape
    spot = [jax.random.randint(jax.random.fold_in(rng, axis), (), 0, dims[axis]) for axis in range(len(dims))]
    array = array.at[tuple(spot)].set(least)
    longest = dims.index(max(dims))
    spot[longest] = (spot[longest] + 1) % dims[longest]
    return array.at[tuple(spot)].set(largest)


def shard_levels(own_key, shape, cuts, least, largest):
    gain, own = 1.0, jax.random.fold_in(own_key, 6)
    for axis_at, blocks in cuts:
        heights = jnp.exp(jax.random.uniform(jax.random.fold_in(own, axis_at), (blocks,), jnp.float32, least / len(cuts), largest / len(cuts)))
        gain = gain * jnp.repeat(heights, shape[axis_at] // blocks).reshape([-1 if axis == axis_at else 1 for axis in range(len(shape))])
    return gain


def bell_draw(own_key, dims, width, limit, cuts=(), kind=jnp.bfloat16):
    array = width * jax.random.normal(own_key, dims, jnp.float32)
    if cuts:
        array = array * shard_levels(own_key, dims, cuts, -0.22, 0.18)
    return jnp.clip(array, -limit, limit).astype(kind)


def setup_inputs(seed: int = 0) -> dict:
    seeds = jax.random.split(jax.random.key(seed), 7)
    return {
        "user_emb": bell_draw(seeds[0], (USERS, E), 1.0, 6.0, ((0, 64),)),
        "camp_emb": bell_draw(seeds[1], (CAMPAIGNS, E), E ** -0.5, 0.375, ((0, 256),)),
        "block_ids": draw_block_ids(jax.random.fold_in(seeds[6], 71), 0),
        "block_count": draw_block_count(jax.random.fold_in(seeds[6], 71), 0),
        "capacity": plant(jax.random.randint(seeds[4], (CAMPAIGNS,), SLOTS * N_USERS * BLOCK // (16 * CBLOCKS), SLOTS * N_USERS * BLOCK // (3 * CBLOCKS) + 1), jax.random.fold_in(seeds[4], 1), SLOTS * N_USERS * BLOCK // (16 * CBLOCKS), (SLOTS * N_USERS * BLOCK // (3 * CBLOCKS) + 1) - 1).astype(jnp.int32),
        "user_limit": plant(jax.random.randint(seeds[5], (USERS,), SLOTS * N_CAMP * BLOCK // (16 * UBLOCKS), SLOTS * N_CAMP * BLOCK // (3 * UBLOCKS) + 1), jax.random.fold_in(seeds[5], 1), SLOTS * N_CAMP * BLOCK // (16 * UBLOCKS), (SLOTS * N_CAMP * BLOCK // (3 * UBLOCKS) + 1) - 1).astype(jnp.int32),
    }


def reference(user_emb, camp_emb, block_ids, block_count, capacity, user_limit):
    nu = N_USERS
    nc = N_CAMP
    ub = U_DEV // BLOCK
    cb = C_GROUP // BLOCK
    users = user_emb.reshape(nu, ub, BLOCK, E)
    camps = camp_emb.reshape(nc, cb, BLOCK, E)
    ids = block_ids.reshape(nc, nu, SLOTS)
    ublk = ids // cb
    cblk = ids % cb
    live = (jnp.arange(SLOTS, dtype=jnp.int32)[None, None, :] < block_count[:, :, None]).astype(jnp.float32)
    devices = jnp.arange(nc * nu, dtype=jnp.int32)

    def score_dev(d):
        j = d // nu
        i = d % nu
        ue = users[i][ublk[j, i]].astype(jnp.float32)
        ce = camps[j][cblk[j, i]].astype(jnp.float32)
        return jnp.einsum("sue,sce->suc", ue, ce, precision=lax.Precision.HIGHEST).astype(jnp.bfloat16)

    scores = lax.map(score_dev, devices)
    cap = capacity.astype(jnp.float32).reshape(nc, cb, BLOCK)
    lim = user_limit.astype(jnp.float32).reshape(nu, ub, BLOCK)
    lam = jnp.zeros((nc, cb, BLOCK), jnp.float32)
    mu = jnp.zeros((nu, ub, BLOCK), jnp.float32)
    lam_bar = lam
    mu_bar = mu
    load = lam
    value = mu
    for step in range(ITERS):
        def sums_dev(d):
            j = d // nu
            i = d % nu
            s_val = scores[d].astype(jnp.float32)
            onehot_c = (cblk[j, i][:, None] == jnp.arange(cb, dtype=jnp.int32)[None, :]).astype(jnp.float32)
            onehot_u = (ublk[j, i][:, None] == jnp.arange(ub, dtype=jnp.int32)[None, :]).astype(jnp.float32)
            lam_rows = lam_bar[j][cblk[j, i]]
            mu_rows = mu_bar[i][ublk[j, i]]
            alloc = jnp.clip(s_val - lam_rows[:, None, :] - mu_rows[:, :, None], 0.0, 1.0) * live[j, i][:, None, None]
            hp = lax.Precision.HIGHEST
            loadp = jnp.einsum("sk,sb->kb", onehot_c, alloc.sum(1), precision=hp)
            rowp = jnp.einsum("sk,sb->kb", onehot_u, alloc.sum(2), precision=hp)
            valp = jnp.einsum("sk,sb->kb", onehot_u, (alloc * s_val).sum(2), precision=hp)
            return loadp, rowp, valp

        loadp, rowp, valp = lax.map(sums_dev, devices)
        load = loadp.reshape(nc, nu, cb, BLOCK).sum(1)
        rows = rowp.reshape(nc, nu, ub, BLOCK).sum(0)
        value = valp.reshape(nc, nu, ub, BLOCK).sum(0)
        lam_new = jnp.maximum(0.0, lam + (load - cap) / cap)
        mu_new = jnp.maximum(0.0, mu + (rows - lim) / lim)
        lam_bar = 2.0 * lam_new - lam
        mu_bar = 2.0 * mu_new - mu
        lam = lam_new
        mu = mu_new
    return (lam.reshape(CAMPAIGNS), mu.reshape(USERS), (load / cap).reshape(CAMPAIGNS), (value / lim).reshape(USERS))
```

```python
import jax
import jax.numpy as jnp
from jax import lax
from jax.experimental import pallas as pl
from jax.experimental.pallas import tpu as pltpu
from jax.sharding import Mesh, PartitionSpec as P

BLOCK = 128
E = 256
SLOTS = 256
UB = 64
CB = 32
NZ, NX, NCORE, NCAMP = 8, 4, 2, 4
UNROLL = 4
F32 = jnp.float32


def _diagonal():
    row = lax.broadcasted_iota(jnp.int32, (BLOCK, BLOCK), 0)
    col = lax.broadcasted_iota(jnp.int32, (BLOCK, BLOCK), 1)
    return row == col


def _clear(lacc, racc):
    lacc[...] = jnp.zeros_like(lacc)
    racc[...] = jnp.zeros_like(racc)


def _slots(ids, count, one):
    cnt = count[0, 0]

    def turn(g, carry):
        for k in range(UNROLL):
            slot = g * UNROLL + k
            code = ids[0, slot]
            ub = code >> 5
            cb = code & (CB - 1)
            live = slot < cnt
            one(slot, ub, cb, jnp.where(live, ub, UB), jnp.where(live, cb, CB))
        return carry

    lax.fori_loop(0, (cnt + UNROLL - 1) // UNROLL, turn, 0)


def _fold(x):
    return x.reshape(BLOCK // 8, 8, BLOCK).sum(0)


def _finish_load(lacc, keep, give, core):
    eye = _diagonal()

    def row(b):
        total = jnp.sum(lacc[b], axis=1, keepdims=True)
        return jnp.sum(jnp.where(eye, total, 0.0), axis=0, keepdims=True)

    half = CB // 2

    def turn(b, carry):
        keep[pl.ds(b, 1), :] = row(core * half + b)
        give[pl.ds(b, 1), :] = row((1 - core) * half + b)
        return carry

    lax.fori_loop(0, half, turn, 0, unroll=2)


def first_kernel(core, ids, count, users, camps, scores, keep, give, rows, lacc, racc):
    _clear(lacc, racc)

    def one(slot, ub, cb, to_u, to_c):
        s = lax.dot_general(
            camps[cb], users[ub], (((1,), (1,)), ((), ())), preferred_element_type=F32
        ).astype(jnp.bfloat16)
        scores[slot] = s
        x = jnp.clip(s.astype(F32), 0.0, 1.0)
        lacc[to_c] += x
        racc[to_u] += _fold(x)

    _slots(ids, count, one)
    _finish_load(lacc, keep, give, core[0])
    rows[...] = racc[:UB].sum(axis=1)


def _load_of(own, other, core):
    a, b = own[...], other[...]
    first = core == 0
    return jnp.concatenate([jnp.where(first, a, b), jnp.where(first, b, a)], axis=0)


def _duals(core, own, other, r0, r1, r2, r3, cap_i, lim_i, lam_in, mu_in):
    load = _load_of(own, other, core)
    rows = (r0[...] + r2[...]) + (r1[...] + r3[...])
    cap = cap_i[...].astype(F32)
    lim = lim_i[...].astype(F32)
    lam_new = jnp.maximum(0.0, lam_in + (load - cap) / cap)
    mu_new = jnp.maximum(0.0, mu_in + (rows - lim) / lim)
    return load, cap, lim, lam_new, mu_new


def _round_kernel(core, ids, count, scores, own, other, r0, r1, r2, r3, cap_i, lim_i, lam_in, mu_in,
                  keep, give, rows, values, lam_out, mu_out, lacc, racc, vacc, lamb, mub):
    _clear(lacc, racc)
    if vacc is not None:
        vacc[...] = jnp.zeros_like(vacc)
    lam = 0.0 if lam_in is None else lam_in[...]
    mu = 0.0 if mu_in is None else mu_in[...]
    _, _, _, lam_new, mu_new = _duals(core[0], own, other, r0, r1, r2, r3, cap_i, lim_i, lam, mu)
    lam_out[...] = lam_new
    mu_out[...] = mu_new
    lam_bar = 2.0 * lam_new - lam
    mub[:UB] = (2.0 * mu_new - mu)[:, None, :]
    eye = _diagonal()
    for b in range(CB):
        spread = jnp.where(eye, lam_bar[b:b + 1, :], 0.0)
        lamb[b] = jnp.broadcast_to(jnp.sum(spread, axis=1, keepdims=True), (BLOCK, BLOCK))

    def one(slot, ub, cb, to_u, to_c):
        s = scores[slot].astype(F32)
        x = jnp.clip(s - lamb[cb] - mub[ub], 0.0, 1.0)
        lacc[to_c] += x
        racc[to_u] += _fold(x)
        if vacc is not None:
            vacc[to_u] += _fold(x * s)

    _slots(ids, count, one)
    _finish_load(lacc, keep, give, core[0])
    rows[...] = racc[:UB].sum(axis=1)
    if vacc is not None:
        values[...] = vacc[:UB].sum(axis=1)


def second_kernel(core, ids, count, scores, own, other, r0, r1, r2, r3, cap_i, lim_i,
                  keep, give, rows, lam_out, mu_out, lacc, racc, lamb, mub):
    _round_kernel(core, ids, count, scores, own, other, r0, r1, r2, r3, cap_i, lim_i, None, None,
                  keep, give, rows, None, lam_out, mu_out, lacc, racc, None, lamb, mub)


def third_kernel(core, ids, count, scores, own, other, r0, r1, r2, r3, cap_i, lim_i, lam_in, mu_in,
                 keep, give, out, lam_out, mu_out, lacc, racc, vacc, lamb, mub):
    _round_kernel(core, ids, count, scores, own, other, r0, r1, r2, r3, cap_i, lim_i, lam_in, mu_in,
                  keep, give, out.at[0], out.at[1], lam_out, mu_out, lacc, racc, vacc, lamb, mub)


def last_kernel(core, own, other, p0, p1, p2, p3, cap_i, lim_i, lam_in, mu_in, duals, user_duals, ratio, user_value):
    load, cap, lim, lam_new, mu_new = _duals(
        core[0], own, other, p0.at[0], p1.at[0], p2.at[0], p3.at[0], cap_i, lim_i, lam_in[...], mu_in[...])
    duals[...] = lam_new
    user_duals[...] = mu_new
    ratio[...] = load / cap
    user_value[...] = ((p0[1] + p2[1]) + (p1[1] + p3[1])) / lim


SMEM = pl.BlockSpec(memory_space=pltpu.SMEM)
VMEM = pl.BlockSpec(memory_space=pltpu.VMEM)


def _call(kernel, n_smem, args, outs, scratch=()):
    return pl.pallas_call(
        kernel,
        in_specs=[SMEM] * n_smem + [VMEM] * (len(args) - n_smem),
        out_specs=[VMEM] * len(outs),
        out_shape=[jax.ShapeDtypeStruct(s, d) for s, d in outs],
        scratch_shapes=[pltpu.VMEM(s, F32) for s in scratch],
        compiler_params=pltpu.CompilerParams(vmem_limit_bytes=40 * 2 ** 20),
    )(*args)


LACC = (CB + 1, BLOCK, BLOCK)
RACC = (UB + 1, 8, BLOCK)
HALF = ((CB // 2, BLOCK), F32)
ROWS = ((UB, BLOCK), F32)
LAM = ((CB, BLOCK), F32)
MUB = (UB, 1, BLOCK)
LAMB = (CB, BLOCK, BLOCK)


def _spread(x, axes, n):
    return lax.all_to_all(jnp.broadcast_to(x[None], (n,) + x.shape), axes, 0, 0, tiled=True)


def _swap(x):
    return lax.ppermute(x, "core", [(0, 1), (1, 0)])


def _sum_load(keep, give):
    own = keep + _swap(give)
    own = _spread(own, ("z", "x"), NZ * NX).sum(0)
    return own, _swap(own)


def _shift(x, k):
    return lax.ppermute(x, "camp", [((i + k) % NCAMP, i) for i in range(NCAMP)])


def _camp_parts(x):
    return x, _shift(x, 1), _shift(x, 2), _shift(x, 3)


def shards(user_emb, camp_emb, block_ids, block_count, capacity, user_limit):
    core = lax.axis_index("core")
    cap = capacity.reshape(CB, BLOCK)
    lim = user_limit.reshape(UB, BLOCK)
    users = user_emb.reshape(UB, BLOCK, E)

    part = _spread(camp_emb, "z", NZ)
    part = _spread(part.reshape(NZ, 64, E), "x", NX).reshape(NX, NZ, 64, E)
    peer = _swap(part)
    first = core == 0
    both = jnp.stack([jnp.where(first, part, peer), jnp.where(first, peer, part)], axis=2)
    camps = both.transpose(1, 0, 2, 3, 4).reshape(CB, BLOCK, E)

    where = jnp.reshape(core, (1,)).astype(jnp.int32)
    slots = (where, block_ids, block_count)
    scores, keep, give, rows = _call(
        first_kernel, 3, (*slots, users, camps),
        [((SLOTS, BLOCK, BLOCK), jnp.bfloat16), HALF, HALF, ROWS], [LACC, RACC])
    parts = _camp_parts(rows)
    own, other = _sum_load(keep, give)
    keep, give, rows, lam, mu = _call(
        second_kernel, 3, (*slots, scores, own, other, *parts, cap, lim),
        [HALF, HALF, ROWS, LAM, ROWS], [LACC, RACC, LAMB, MUB])
    parts = _camp_parts(rows)
    own, other = _sum_load(keep, give)
    keep, give, both_sums, lam, mu = _call(
        third_kernel, 3, (*slots, scores, own, other, *parts, cap, lim, lam, mu),
        [HALF, HALF, ((2, UB, BLOCK), F32), LAM, ROWS], [LACC, RACC, RACC, LAMB, MUB])
    parts = _camp_parts(both_sums)
    own, other = _sum_load(keep, give)
    duals, user_duals, ratio, value = _call(
        last_kernel, 1, (where, own, other, *parts, cap, lim, lam, mu), [LAM, ROWS, LAM, ROWS])
    return duals.reshape(-1), user_duals.reshape(-1), ratio.reshape(-1), value.reshape(-1)


def solution(mesh):
    fine = Mesh(mesh.devices.reshape(NZ, NX, NCORE, NCAMP), ("z", "x", "core", "camp"))
    users = ("z", "x", "core")
    return jax.shard_map(
        shards,
        mesh=fine,
        in_specs=(P(users, None), P(("camp",) + users, None), P("camp", users), P("camp", users), P("camp"), P(users)),
        out_specs=(P("camp"), P(users), P("camp"), P(users)),
        check_vma=False,
    )
```

```python
import jax
import jax.numpy as jnp
from jax import lax
from jax.experimental import pallas as pl
from jax.experimental.pallas import tpu as pltpu
from jax.sharding import Mesh, PartitionSpec as P

BLOCK = 128
E = 256
SLOTS = 256
UB = 64
CB = 32
NZ, NX, NCORE, NCAMP = 8, 4, 2, 4
UNROLL = 4
GROUP = 32
LIMIT = 20 * 2 ** 20
F32 = jnp.float32


def _clear(lacc, racc):
    lacc[...] = jnp.zeros_like(lacc)
    racc[...] = jnp.zeros_like(racc)


def _slots(ids, count, one):
    cnt = count[0, 0]

    def turn(g, carry):
        for k in range(UNROLL):
            slot = g * UNROLL + k
            code = ids[0, slot]
            ub = code >> 5
            cb = code & (CB - 1)
            live = slot < cnt
            one(slot, ub, cb, jnp.where(live, ub, UB), jnp.where(live, cb, CB))
        return carry

    lax.fori_loop(0, (cnt + UNROLL - 1) // UNROLL, turn, 0)


def _fold(x):
    return x.reshape(BLOCK // 8, 8, BLOCK).sum(0)


def _finish_load(lacc, keep, give, core):
    half = CB // 2

    def row(b):
        return jnp.sum(lacc[b].T, axis=0, keepdims=True)

    def turn(b, carry):
        keep[pl.ds(b, 1), :] = row(core * half + b)
        give[pl.ds(b, 1), :] = row((1 - core) * half + b)
        return carry

    lax.fori_loop(0, half, turn, 0, unroll=4)


def _group(ids, cnt, g, size):
    out = []
    for k in range(size):
        slot = g * size + k
        code = ids[0, slot]
        out.append((slot, code >> 5, code & (CB - 1), slot < cnt))
    return out


def first_kernel(core, ids, count, users, camps, scores, keep, give, rows, lacc, racc):
    _clear(lacc, racc)
    cnt = count[0, 0]
    turns = (cnt + GROUP - 1) // GROUP

    def products(g):
        return [
            lax.dot_general(
                camps[cb], users[ub], (((1,), (1,)), ((), ())), preferred_element_type=F32
            ).astype(jnp.bfloat16)
            for _, ub, cb, _ in _group(ids, cnt, g, GROUP)
        ]

    def store(g, blocks):
        for k, block in enumerate(blocks):
            scores[g * GROUP + k] = block

    def add(g):
        for slot, ub, cb, live in _group(ids, cnt, g, GROUP):
            x = jnp.clip(scores[slot].astype(F32), 0.0, 1.0)
            lacc[jnp.where(live, cb, CB)] += x
            racc[jnp.where(live, ub, UB)] += _fold(x)

    store(0, products(0))

    def turn(g, carry):
        blocks = products(g)
        add(g - 1)
        store(g, blocks)
        return carry

    lax.fori_loop(1, turns, turn, 0)
    add(turns - 1)
    _finish_load(lacc, keep, give, core[0])
    rows[...] = racc[:UB].sum(axis=1)


def fetch_kernel(users, out, sem):
    copy = pltpu.make_async_copy(users, out, sem)
    copy.start()
    copy.wait()


def _fetch(users):
    return pl.pallas_call(
        fetch_kernel,
        in_specs=[pl.BlockSpec(memory_space=pl.ANY)],
        out_specs=VMEM,
        out_shape=jax.ShapeDtypeStruct(users.shape, users.dtype),
        scratch_shapes=[pltpu.SemaphoreType.DMA],
        compiler_params=pltpu.CompilerParams(vmem_limit_bytes=LIMIT),
        cost_estimate=pl.CostEstimate(flops=0, bytes_accessed=2 * users.size * 2, transcendentals=0),
    )(users)


def _load_of(own, other, core):
    a, b = own[...], other[...]
    first = core == 0
    return jnp.concatenate([jnp.where(first, a, b), jnp.where(first, b, a)], axis=0)


def _duals(core, own, other, r0, r1, r2, r3, cap_i, lim_i, lam_in, mu_in):
    load = _load_of(own, other, core)
    rows = (r0[...] + r2[...]) + (r1[...] + r3[...])
    cap = cap_i[...].astype(F32)
    lim = lim_i[...].astype(F32)
    lam_new = jnp.maximum(0.0, lam_in + (load - cap) / cap)
    mu_new = jnp.maximum(0.0, mu_in + (rows - lim) / lim)
    return load, cap, lim, lam_new, mu_new


def _round_kernel(core, ids, count, scores, own, other, r0, r1, r2, r3, cap_i, lim_i, lam_in, mu_in,
                  keep, give, rows, values, lam_out, mu_out, lacc, racc, vacc, lamb, mub):
    _clear(lacc, racc)
    if vacc is not None:
        vacc[...] = jnp.zeros_like(vacc)
    lam = 0.0 if lam_in is None else lam_in[...]
    mu = 0.0 if mu_in is None else mu_in[...]
    _, _, _, lam_new, mu_new = _duals(core[0], own, other, r0, r1, r2, r3, cap_i, lim_i, lam, mu)
    lam_out[...] = lam_new
    mu_out[...] = mu_new
    lam_bar = 2.0 * lam_new - lam
    mub[:UB] = (2.0 * mu_new - mu)[:, None, :]
    for b in range(CB):
        lamb[b] = jnp.broadcast_to(lam_bar[b:b + 1, :], (BLOCK, BLOCK)).T

    def one(slot, ub, cb, to_u, to_c):
        s = scores[slot].astype(F32)
        x = jnp.clip(s - lamb[cb] - mub[ub], 0.0, 1.0)
        lacc[to_c] += x
        racc[to_u] += _fold(x)
        if vacc is not None:
            vacc[to_u] += _fold(x * s)

    _slots(ids, count, one)
    _finish_load(lacc, keep, give, core[0])
    rows[...] = racc[:UB].sum(axis=1)
    if vacc is not None:
        values[...] = vacc[:UB].sum(axis=1)


def second_kernel(core, ids, count, scores, own, other, r0, r1, r2, r3, cap_i, lim_i,
                  keep, give, rows, lam_out, mu_out, lacc, racc, lamb, mub):
    _round_kernel(core, ids, count, scores, own, other, r0, r1, r2, r3, cap_i, lim_i, None, None,
                  keep, give, rows, None, lam_out, mu_out, lacc, racc, None, lamb, mub)


def third_kernel(core, ids, count, scores, own, other, r0, r1, r2, r3, cap_i, lim_i, lam_in, mu_in,
                 keep, give, out, lam_out, mu_out, lacc, racc, vacc, lamb, mub):
    _round_kernel(core, ids, count, scores, own, other, r0, r1, r2, r3, cap_i, lim_i, lam_in, mu_in,
                  keep, give, out.at[0], out.at[1], lam_out, mu_out, lacc, racc, vacc, lamb, mub)


def last_kernel(core, own, other, p0, p1, p2, p3, cap_i, lim_i, lam_in, mu_in, duals, user_duals, ratio, user_value):
    load, cap, lim, lam_new, mu_new = _duals(
        core[0], own, other, p0.at[0], p1.at[0], p2.at[0], p3.at[0], cap_i, lim_i, lam_in[...], mu_in[...])
    duals[...] = lam_new
    user_duals[...] = mu_new
    ratio[...] = load / cap
    user_value[...] = ((p0[1] + p2[1]) + (p1[1] + p3[1])) / lim


SMEM = pl.BlockSpec(memory_space=pltpu.SMEM)
VMEM = pl.BlockSpec(memory_space=pltpu.VMEM)


def _call(kernel, n_smem, args, outs, scratch=()):
    return pl.pallas_call(
        kernel,
        in_specs=[SMEM] * n_smem + [VMEM] * (len(args) - n_smem),
        out_specs=[VMEM] * len(outs),
        out_shape=[jax.ShapeDtypeStruct(s, d) for s, d in outs],
        scratch_shapes=[pltpu.VMEM(s, F32) for s in scratch],
        compiler_params=pltpu.CompilerParams(vmem_limit_bytes=LIMIT),
    )(*args)


LACC = (CB + 1, BLOCK, BLOCK)
RACC = (UB + 1, 8, BLOCK)
HALF = ((CB // 2, BLOCK), F32)
ROWS = ((UB, BLOCK), F32)
LAM = ((CB, BLOCK), F32)
MUB = (UB, 1, BLOCK)
LAMB = (CB, BLOCK, BLOCK)


def _spread(x, axes, n):
    return lax.all_to_all(jnp.broadcast_to(x[None], (n,) + x.shape), axes, 0, 0, tiled=True)


def _swap(x):
    return lax.ppermute(x, "core", [(0, 1), (1, 0)])


def _sum_load(keep, give):
    own = keep + _swap(give)
    own = _spread(own, ("z", "x"), NZ * NX).sum(0)
    return own, _swap(own)


def _shift(x, k):
    return lax.ppermute(x, "camp", [((i + k) % NCAMP, i) for i in range(NCAMP)])


def _camp_parts(x):
    return x, _shift(x, 1), _shift(x, 2), _shift(x, 3)


def shards(user_emb, camp_emb, block_ids, block_count, capacity, user_limit):
    core = lax.axis_index("core")
    cap = capacity.reshape(CB, BLOCK)
    lim = user_limit.reshape(UB, BLOCK)
    users = user_emb.reshape(UB, BLOCK, E)

    part = _spread(camp_emb, "z", NZ)
    part, users = lax.optimization_barrier((part, users))
    users = _fetch(users)
    part = _spread(part.reshape(NZ, 64, E), "x", NX).reshape(NX, NZ, 64, E)
    peer = _swap(part)
    first = core == 0
    both = jnp.stack([jnp.where(first, part, peer), jnp.where(first, peer, part)], axis=2)
    camps = both.transpose(1, 0, 2, 3, 4).reshape(CB, BLOCK, E)

    where = jnp.reshape(core, (1,)).astype(jnp.int32)
    slots = (where, block_ids, block_count)
    scores, keep, give, rows = _call(
        first_kernel, 3, (*slots, users, camps),
        [((SLOTS, BLOCK, BLOCK), jnp.bfloat16), HALF, HALF, ROWS], [LACC, RACC])
    parts = _camp_parts(rows)
    own, other = _sum_load(keep, give)
    keep, give, rows, lam, mu = _call(
        second_kernel, 3, (*slots, scores, own, other, *parts, cap, lim),
        [HALF, HALF, ROWS, LAM, ROWS], [LACC, RACC, LAMB, MUB])
    parts = _camp_parts(rows)
    own, other = _sum_load(keep, give)
    keep, give, both_sums, lam, mu = _call(
        third_kernel, 3, (*slots, scores, own, other, *parts, cap, lim, lam, mu),
        [HALF, HALF, ((2, UB, BLOCK), F32), LAM, ROWS], [LACC, RACC, RACC, LAMB, MUB])
    parts = _camp_parts(both_sums)
    own, other = _sum_load(keep, give)
    duals, user_duals, ratio, value = _call(
        last_kernel, 1, (where, own, other, *parts, cap, lim, lam, mu), [LAM, ROWS, LAM, ROWS])
    return duals.reshape(-1), user_duals.reshape(-1), ratio.reshape(-1), value.reshape(-1)


def solution(mesh):
    fine = Mesh(mesh.devices.reshape(NZ, NX, NCORE, NCAMP), ("z", "x", "core", "camp"))
    users = ("z", "x", "core")
    return jax.shard_map(
        shards,
        mesh=fine,
        in_specs=(P(users, None), P(("camp",) + users, None), P("camp", users), P("camp", users), P("camp"), P(users)),
        out_specs=(P("camp"), P(users), P("camp"), P(users)),
        check_vma=False,
    )
```

```python
import jax
import jax.numpy as jnp
from jax import lax
from jax.experimental import pallas as pl
from jax.experimental.pallas import tpu as pltpu
from jax.sharding import Mesh, PartitionSpec as P

BLOCK = 128
E = 256
SLOTS = 256
UB = 64
CB = 32
NZ, NX, NCORE, NCAMP = 8, 4, 2, 4
UNROLL = 4
GROUP = 32
WIDE = 50
F32 = jnp.float32


def _clear(lacc, racc):
    lacc[...] = jnp.zeros_like(lacc)
    racc[...] = jnp.zeros_like(racc)


def _chunk(src, dst, sems, g):
    at = pl.ds(g * GROUP, GROUP)
    return pltpu.make_async_copy(src.at[at], dst.at[at], sems.at[g])


def _each(turns, do):
    def turn(g, carry):
        do(g)
        return carry

    lax.fori_loop(0, turns, turn, 0)


def _fold(x):
    return x.reshape(BLOCK // 8, 8, BLOCK).sum(0)


def _finish_load(lacc, keep, give, core):
    half = CB // 2

    def row(b):
        return jnp.sum(lacc[b].T, axis=0, keepdims=True)

    def turn(b, carry):
        keep[pl.ds(b, 1), :] = row(core * half + b)
        give[pl.ds(b, 1), :] = row((1 - core) * half + b)
        return carry

    lax.fori_loop(0, half, turn, 0, unroll=4)


def _group(ids, cnt, first, size):
    out = []
    for k in range(size):
        slot = first + k
        code = ids[0, slot]
        out.append((slot, code >> 5, code & (CB - 1), slot < cnt))
    return out


def first_kernel(core, ids, count, part, peer, users_in, kept, keep, give, rows, lacc, racc, panel, users, scores,
                 sems, fetched, stored):
    me = core[0]
    fetch = pltpu.make_async_copy(users_in, users, fetched)
    fetch.start()
    copies = [
        pltpu.make_async_copy(src.at[x], panel.at[:, x, half], sems.at[x, k])
        for x in range(NX)
        for k, (src, half) in enumerate(((part, me), (peer, 1 - me)))
    ]
    for copy in copies:
        copy.start()
    _clear(lacc, racc)
    for copy in copies:
        copy.wait()
    fetch.wait()
    camps = panel.reshape(CB, BLOCK, E)
    cnt = count[0, 0]
    turns = (cnt + GROUP - 1) // GROUP

    def products(g):
        return [
            lax.dot_general(
                camps[cb], users[ub], (((1,), (1,)), ((), ())), preferred_element_type=F32
            ).astype(jnp.bfloat16)
            for _, ub, cb, _ in _group(ids, cnt, g * GROUP, GROUP)
        ]

    def store(g, blocks):
        for k, block in enumerate(blocks):
            scores[g * GROUP + k] = block
        _chunk(scores, kept, stored, g).start()

    def add(g):
        for slot, ub, cb, live in _group(ids, cnt, g * GROUP, GROUP):
            x = jnp.clip(scores[slot].astype(F32), 0.0, 1.0)
            lacc[jnp.where(live, cb, CB)] += x
            racc[jnp.where(live, ub, UB)] += _fold(x)

    store(0, products(0))

    def turn(g, carry):
        blocks = products(g)
        add(g - 1)
        store(g, blocks)
        return carry

    lax.fori_loop(1, turns, turn, 0)
    add(turns - 1)
    _finish_load(lacc, keep, give, core[0])
    rows[...] = racc[:UB].sum(axis=1)
    _each(turns, lambda g: _chunk(scores, kept, stored, g).wait())


def _load_of(own, other, core):
    a, b = own[...], other[...]
    first = core == 0
    return jnp.concatenate([jnp.where(first, a, b), jnp.where(first, b, a)], axis=0)


def _duals(core, own, other, r0, r1, r2, r3, cap_i, lim_i, lam_in, mu_in):
    load = _load_of(own, other, core)
    rows = (r0[...] + r2[...]) + (r1[...] + r3[...])
    cap = cap_i[...].astype(F32)
    lim = lim_i[...].astype(F32)
    lam_new = jnp.maximum(0.0, lam_in + (load - cap) / cap)
    mu_new = jnp.maximum(0.0, mu_in + (rows - lim) / lim)
    return load, cap, lim, lam_new, mu_new


def _round_kernel(core, ids, count, kept, own, other, r0, r1, r2, r3, cap_i, lim_i, lam_in, mu_in,
                  keep, give, rows, values, lam_out, mu_out, lacc, racc, vacc, lamb, mub, scores, loaded):
    cnt = count[0, 0]
    turns = (cnt + GROUP - 1) // GROUP
    _each(turns, lambda g: _chunk(kept, scores, loaded, g).start())
    _clear(lacc, racc)
    if vacc is not None:
        vacc[...] = jnp.zeros_like(vacc)
    lam = 0.0 if lam_in is None else lam_in[...]
    mu = 0.0 if mu_in is None else mu_in[...]
    _, _, _, lam_new, mu_new = _duals(core[0], own, other, r0, r1, r2, r3, cap_i, lim_i, lam, mu)
    lam_out[...] = lam_new
    mu_out[...] = mu_new
    lam_bar = 2.0 * lam_new - lam
    mub[:UB] = (2.0 * mu_new - mu)[:, None, :]
    for b in range(CB):
        lamb[b] = jnp.broadcast_to(lam_bar[b:b + 1, :], (BLOCK, BLOCK)).T

    def some(first):
        for slot, ub, cb, live in _group(ids, cnt, first, UNROLL):
            s = scores[slot].astype(F32)
            x = jnp.clip(s - lamb[cb] - mub[ub], 0.0, 1.0)
            lacc[jnp.where(live, cb, CB)] += x
            to_u = jnp.where(live, ub, UB)
            racc[to_u] += _fold(x)
            if vacc is not None:
                vacc[to_u] += _fold(x * s)

    def chunk(g):
        _chunk(kept, scores, loaded, g).wait()
        _each(GROUP // UNROLL, lambda i: some(g * GROUP + i * UNROLL))

    _each(turns, chunk)
    _finish_load(lacc, keep, give, core[0])
    rows[...] = racc[:UB].sum(axis=1)
    if vacc is not None:
        values[...] = vacc[:UB].sum(axis=1)


def second_kernel(core, ids, count, own, other, r0, r1, r2, r3, cap_i, lim_i, kept,
                  keep, give, rows, lam_out, mu_out, lacc, racc, lamb, mub, scores, loaded):
    _round_kernel(core, ids, count, kept, own, other, r0, r1, r2, r3, cap_i, lim_i, None, None,
                  keep, give, rows, None, lam_out, mu_out, lacc, racc, None, lamb, mub, scores, loaded)


def third_kernel(core, ids, count, own, other, r0, r1, r2, r3, cap_i, lim_i, lam_in, mu_in, kept,
                 keep, give, out, lam_out, mu_out, lacc, racc, vacc, lamb, mub, scores, loaded):
    _round_kernel(core, ids, count, kept, own, other, r0, r1, r2, r3, cap_i, lim_i, lam_in, mu_in,
                  keep, give, out.at[0], out.at[1], lam_out, mu_out, lacc, racc, vacc, lamb, mub, scores, loaded)


def last_kernel(core, own, other, p0, p1, p2, p3, cap_i, lim_i, lam_in, mu_in, duals, user_duals, ratio, user_value):
    load, cap, lim, lam_new, mu_new = _duals(
        core[0], own, other, p0.at[0], p1.at[0], p2.at[0], p3.at[0], cap_i, lim_i, lam_in[...], mu_in[...])
    duals[...] = lam_new
    user_duals[...] = mu_new
    ratio[...] = load / cap
    user_value[...] = ((p0[1] + p2[1]) + (p1[1] + p3[1])) / lim


SMEM = pl.BlockSpec(memory_space=pltpu.SMEM)
VMEM = pl.BlockSpec(memory_space=pltpu.VMEM)
ANY = pl.BlockSpec(memory_space=pl.ANY)


def _call(kernel, n_smem, args, outs, scratch=(), more=(), any_in=0, any_out=0, limit=20):
    return pl.pallas_call(
        kernel,
        in_specs=[SMEM] * n_smem + [VMEM] * (len(args) - n_smem - any_in) + [ANY] * any_in,
        out_specs=[ANY] * any_out + [VMEM] * (len(outs) - any_out),
        out_shape=[jax.ShapeDtypeStruct(s, d) for s, d in outs],
        scratch_shapes=[pltpu.VMEM(s, F32) for s in scratch] + list(more),
        compiler_params=pltpu.CompilerParams(vmem_limit_bytes=limit * 2 ** 20),
    )(*args)


LACC = (CB + 1, BLOCK, BLOCK)
RACC = (UB + 1, 8, BLOCK)
HALF = ((CB // 2, BLOCK), F32)
ROWS = ((UB, BLOCK), F32)
LAM = ((CB, BLOCK), F32)
MUB = (UB, 1, BLOCK)
SCORES = ((SLOTS, BLOCK, BLOCK), jnp.bfloat16)
CHUNKS = [pltpu.VMEM(*SCORES), pltpu.SemaphoreType.DMA((SLOTS // GROUP,))]
LAMB = (CB, BLOCK, BLOCK)


def _spread(x, axes, n):
    return lax.all_to_all(jnp.broadcast_to(x[None], (n,) + x.shape), axes, 0, 0, tiled=True)


def _swap(x):
    return lax.ppermute(x, "core", [(0, 1), (1, 0)])


def spread_kernel(keep, got, out):
    out[...] = jnp.broadcast_to((keep[...] + got[...])[None], out.shape)


def sum_kernel(parts, out):
    out[...] = parts[...].sum(0)


def _sum_load(keep, give):
    (wide,) = _call(spread_kernel, 0, (keep, _swap(give)), [((NZ * NX,) + HALF[0], F32)])
    wide = lax.all_to_all(wide, ("z", "x"), 0, 0, tiled=True)
    (own,) = _call(sum_kernel, 0, (wide,), [HALF])
    return own, _swap(own)


def _shift(x, k):
    return lax.ppermute(x, "camp", [((i + k) % NCAMP, i) for i in range(NCAMP)])


def _camp_parts(x):
    return x, _shift(x, 1), _shift(x, 2), _shift(x, 3)


def shards(user_emb, camp_emb, block_ids, block_count, capacity, user_limit):
    where = jnp.reshape(lax.axis_index("core"), (1,)).astype(jnp.int32)
    camp_emb, where = lax.optimization_barrier((camp_emb, where))
    cap = capacity.reshape(CB, BLOCK)
    lim = user_limit.reshape(UB, BLOCK)
    users = user_emb.reshape(UB, BLOCK, E)

    part = _spread(camp_emb, "z", NZ)
    part = _spread(part.reshape(NZ, 64, E), "x", NX).reshape(NX, NZ, 64, E)
    peer = _swap(part)

    slots = (where, block_ids, block_count)
    kept, keep, give, rows = _call(
        first_kernel, 3, (*slots, part, peer, users), [SCORES, HALF, HALF, ROWS], [LACC, RACC],
        [pltpu.VMEM((NZ, NX, 2, 64, E), jnp.bfloat16), pltpu.VMEM((UB, BLOCK, E), jnp.bfloat16), CHUNKS[0],
         pltpu.SemaphoreType.DMA((NX, 2)), pltpu.SemaphoreType.DMA, CHUNKS[1]], any_in=1, any_out=1, limit=WIDE)
    parts = _camp_parts(rows)
    own, other = _sum_load(keep, give)
    keep, give, rows, lam, mu = _call(
        second_kernel, 3, (*slots, own, other, *parts, cap, lim, kept),
        [HALF, HALF, ROWS, LAM, ROWS], [LACC, RACC, LAMB, MUB], CHUNKS, any_in=1, limit=WIDE)
    parts = _camp_parts(rows)
    own, other = _sum_load(keep, give)
    keep, give, both_sums, lam, mu = _call(
        third_kernel, 3, (*slots, own, other, *parts, cap, lim, lam, mu, kept),
        [HALF, HALF, ((2, UB, BLOCK), F32), LAM, ROWS], [LACC, RACC, RACC, LAMB, MUB], CHUNKS, any_in=1, limit=WIDE)
    parts = _camp_parts(both_sums)
    own, other = _sum_load(keep, give)
    duals, user_duals, ratio, value = _call(
        last_kernel, 1, (where, own, other, *parts, cap, lim, lam, mu), [LAM, ROWS, LAM, ROWS])
    return duals.reshape(-1), user_duals.reshape(-1), ratio.reshape(-1), value.reshape(-1)


def solution(mesh):
    fine = Mesh(mesh.devices.reshape(NZ, NX, NCORE, NCAMP), ("z", "x", "core", "camp"))
    users = ("z", "x", "core")
    return jax.shard_map(
        shards,
        mesh=fine,
        in_specs=(P(users, None), P(("camp",) + users, None), P("camp", users), P("camp", users), P("camp"), P(users)),
        out_specs=(P("camp"), P(users), P("camp"), P(users)),
        check_vma=False,
    )
```

```python
import jax
import jax.numpy as jnp
from jax import lax
from jax.experimental import pallas as pl
from jax.experimental.pallas import tpu as pltpu
from jax.sharding import Mesh, PartitionSpec as P

BLOCK = 128
E = 256
SLOTS = 256
UB = 64
CB = 32
NZ, NX, NCORE, NCAMP = 8, 4, 2, 4
UNROLL = 4
GROUP = 32
WIDE = 50
FIRST = 43
AHEAD = 2
F32 = jnp.float32


def _clear(lacc, racc):
    lacc[...] = jnp.zeros_like(lacc)
    racc[...] = jnp.zeros_like(racc)


def _chunk(src, dst, sems, g):
    at = pl.ds(g * GROUP, GROUP)
    return pltpu.make_async_copy(src.at[at], dst.at[at], sems.at[g])


def _each(turns, do):
    def turn(g, carry):
        do(g)
        return carry

    lax.fori_loop(0, turns, turn, 0)


def _fold(x):
    return x.reshape(BLOCK // 8, 8, BLOCK).sum(0)


def _finish_load(lacc, keep, give, core):
    half = CB // 2

    def row(b):
        return jnp.sum(lacc[b].T, axis=0, keepdims=True)

    def turn(b, carry):
        keep[pl.ds(b, 1), :] = row(core * half + b)
        give[pl.ds(b, 1), :] = row((1 - core) * half + b)
        return carry

    lax.fori_loop(0, half, turn, 0, unroll=4)


def _group(ids, cnt, first, size):
    out = []
    for k in range(size):
        slot = first + k
        code = ids[0, slot]
        out.append((slot, code >> 5, code & (CB - 1), slot < cnt))
    return out


def fetch_kernel(users, out, sem):
    copy = pltpu.make_async_copy(users, out, sem)
    copy.start()
    copy.wait()


def first_kernel(core, count, users, part, peer, codes, kept, keep, give, rows, lacc, racc, panel, scores, ids,
                 sems, fetched, stored):
    me = core[0]
    fetch = pltpu.make_async_copy(codes, ids, fetched)
    fetch.start()
    copies = [
        pltpu.make_async_copy(src.at[x], panel.at[:, x, half], sems.at[x, k])
        for x in range(NX)
        for k, (src, half) in enumerate(((part, me), (peer, 1 - me)))
    ]
    for copy in copies:
        copy.start()
    _clear(lacc, racc)
    for copy in copies:
        copy.wait()
    fetch.wait()
    camps = panel.reshape(CB, BLOCK, E)
    cnt = count[0, 0]
    turns = (cnt + GROUP - 1) // GROUP

    def products(g):
        return [
            lax.dot_general(
                camps[cb], users[ub], (((1,), (1,)), ((), ())), preferred_element_type=F32
            ).astype(jnp.bfloat16)
            for _, ub, cb, _ in _group(ids, cnt, g * GROUP, GROUP)
        ]

    def store(g, blocks):
        for k, block in enumerate(blocks):
            scores[g * GROUP + k] = block
        _chunk(scores, kept, stored, g).start()

    def add(g):
        for slot, ub, cb, live in _group(ids, cnt, g * GROUP, GROUP):
            x = jnp.clip(scores[slot].astype(F32), 0.0, 1.0)
            lacc[jnp.where(live, cb, CB)] += x
            racc[jnp.where(live, ub, UB)] += _fold(x)

    store(0, products(0))

    def turn(g, carry):
        blocks = products(g)
        add(g - 1)
        store(g, blocks)
        return carry

    lax.fori_loop(1, turns, turn, 0)
    add(turns - 1)
    _finish_load(lacc, keep, give, core[0])
    rows[...] = racc[:UB].sum(axis=1)
    _each(turns, lambda g: _chunk(scores, kept, stored, g).wait())


def _load_of(own, other, core):
    a, b = own[...], other[...]
    first = core == 0
    return jnp.concatenate([jnp.where(first, a, b), jnp.where(first, b, a)], axis=0)


def _duals(core, own, other, r0, r1, r2, r3, cap_i, lim_i, lam_in, mu_in):
    load = _load_of(own, other, core)
    rows = (r0[...] + r2[...]) + (r1[...] + r3[...])
    cap = cap_i[...].astype(F32)
    lim = lim_i[...].astype(F32)
    lam_new = jnp.maximum(0.0, lam_in + (load - cap) / cap)
    mu_new = jnp.maximum(0.0, mu_in + (rows - lim) / lim)
    return load, cap, lim, lam_new, mu_new


def _round_kernel(core, ids, count, kept, own, other, r0, r1, r2, r3, cap_i, lim_i, lam_in, mu_in,
                  keep, give, rows, values, lam_out, mu_out, lacc, racc, vacc, lamb, mub, scores, loaded):
    cnt = count[0, 0]
    turns = (cnt + GROUP - 1) // GROUP
    _each(jnp.minimum(turns, AHEAD), lambda g: _chunk(kept, scores, loaded, g).start())
    _clear(lacc, racc)
    if vacc is not None:
        vacc[...] = jnp.zeros_like(vacc)
    lam = 0.0 if lam_in is None else lam_in[...]
    mu = 0.0 if mu_in is None else mu_in[...]
    _, _, _, lam_new, mu_new = _duals(core[0], own, other, r0, r1, r2, r3, cap_i, lim_i, lam, mu)
    lam_out[...] = lam_new
    mu_out[...] = mu_new
    lam_bar = 2.0 * lam_new - lam
    mub[:UB] = (2.0 * mu_new - mu)[:, None, :]
    for b in range(CB):
        lamb[b] = jnp.broadcast_to(lam_bar[b:b + 1, :], (BLOCK, BLOCK)).T

    def some(first):
        for slot, ub, cb, live in _group(ids, cnt, first, UNROLL):
            s = scores[slot].astype(F32)
            x = jnp.clip(s - lamb[cb] - mub[ub], 0.0, 1.0)
            lacc[jnp.where(live, cb, CB)] += x
            to_u = jnp.where(live, ub, UB)
            racc[to_u] += _fold(x)
            if vacc is not None:
                vacc[to_u] += _fold(x * s)

    def chunk(g):
        _chunk(kept, scores, loaded, g).wait()

        @pl.when(g + AHEAD < turns)
        def _():
            _chunk(kept, scores, loaded, g + AHEAD).start()

        _each(GROUP // UNROLL, lambda i: some(g * GROUP + i * UNROLL))

    _each(turns, chunk)
    _finish_load(lacc, keep, give, core[0])
    rows[...] = racc[:UB].sum(axis=1)
    if vacc is not None:
        values[...] = vacc[:UB].sum(axis=1)


def second_kernel(core, ids, count, own, other, r0, r1, r2, r3, cap_i, lim_i, kept,
                  keep, give, rows, lam_out, mu_out, lacc, racc, lamb, mub, scores, loaded):
    _round_kernel(core, ids, count, kept, own, other, r0, r1, r2, r3, cap_i, lim_i, None, None,
                  keep, give, rows, None, lam_out, mu_out, lacc, racc, None, lamb, mub, scores, loaded)


def third_kernel(core, ids, count, own, other, r0, r1, r2, r3, cap_i, lim_i, lam_in, mu_in, kept,
                 keep, give, out, lam_out, mu_out, lacc, racc, vacc, lamb, mub, scores, loaded):
    _round_kernel(core, ids, count, kept, own, other, r0, r1, r2, r3, cap_i, lim_i, lam_in, mu_in,
                  keep, give, out.at[0], out.at[1], lam_out, mu_out, lacc, racc, vacc, lamb, mub, scores, loaded)


def last_kernel(core, own, other, p0, p1, p2, p3, cap_i, lim_i, lam_in, mu_in, duals, user_duals, ratio, user_value):
    load, cap, lim, lam_new, mu_new = _duals(
        core[0], own, other, p0.at[0], p1.at[0], p2.at[0], p3.at[0], cap_i, lim_i, lam_in[...], mu_in[...])
    duals[...] = lam_new
    user_duals[...] = mu_new
    ratio[...] = load / cap
    user_value[...] = ((p0[1] + p2[1]) + (p1[1] + p3[1])) / lim


SMEM = pl.BlockSpec(memory_space=pltpu.SMEM)
VMEM = pl.BlockSpec(memory_space=pltpu.VMEM)
ANY = pl.BlockSpec(memory_space=pl.ANY)


def _call(kernel, n_smem, args, outs, scratch=(), more=(), any_in=0, any_out=0, limit=20):
    return pl.pallas_call(
        kernel,
        in_specs=[SMEM] * n_smem + [VMEM] * (len(args) - n_smem - any_in) + [ANY] * any_in,
        out_specs=[ANY] * any_out + [VMEM] * (len(outs) - any_out),
        out_shape=[jax.ShapeDtypeStruct(s, d) for s, d in outs],
        scratch_shapes=[pltpu.VMEM(s, F32) for s in scratch] + list(more),
        compiler_params=pltpu.CompilerParams(vmem_limit_bytes=limit * 2 ** 20),
    )(*args)


LACC = (CB + 1, BLOCK, BLOCK)
RACC = (UB + 1, 8, BLOCK)
HALF = ((CB // 2, BLOCK), F32)
ROWS = ((UB, BLOCK), F32)
LAM = ((CB, BLOCK), F32)
MUB = (UB, 1, BLOCK)
SCORES = ((SLOTS, BLOCK, BLOCK), jnp.bfloat16)
CHUNKS = [pltpu.VMEM(*SCORES), pltpu.SemaphoreType.DMA((SLOTS // GROUP,))]
LAMB = (CB, BLOCK, BLOCK)


def _spread(x, axes, n):
    return lax.all_to_all(jnp.broadcast_to(x[None], (n,) + x.shape), axes, 0, 0, tiled=True)


def _swap(x):
    return lax.ppermute(x, "core", [(0, 1), (1, 0)])


def spread_kernel(keep, got, out):
    out[...] = jnp.broadcast_to((keep[...] + got[...])[None], out.shape)


def sum_kernel(parts, out):
    out[...] = parts[...].sum(0)


def _sum_load(keep, give):
    (wide,) = _call(spread_kernel, 0, (keep, _swap(give)), [((NZ * NX,) + HALF[0], F32)])
    wide = lax.all_to_all(wide, ("z", "x"), 0, 0, tiled=True)
    (own,) = _call(sum_kernel, 0, (wide,), [HALF])
    return own, _swap(own)


def _shift(x, k):
    return lax.ppermute(x, "camp", [((i + k) % NCAMP, i) for i in range(NCAMP)])


def _camp_parts(x):
    return x, _shift(x, 1), _shift(x, 2), _shift(x, 3)


def shards(user_emb, camp_emb, block_ids, block_count, capacity, user_limit):
    where = jnp.reshape(lax.axis_index("core"), (1,)).astype(jnp.int32)
    camp_emb, where = lax.optimization_barrier((camp_emb, where))
    cap = capacity.reshape(CB, BLOCK)
    lim = user_limit.reshape(UB, BLOCK)
    users = user_emb.reshape(UB, BLOCK, E)

    part = _spread(camp_emb, "z", NZ)
    part = _spread(part.reshape(NZ, 64, E), "x", NX).reshape(NX, NZ, 64, E)
    part, users = lax.optimization_barrier((part, users))
    (users,) = _call(
        fetch_kernel, 0, (users,), [(users.shape, users.dtype)], [], [pltpu.SemaphoreType.DMA], any_in=1, limit=4)
    peer = _swap(part)

    slots = (where, block_ids, block_count)
    kept, keep, give, rows = _call(
        first_kernel, 2, (where, block_count, users, part, peer, block_ids), [SCORES, HALF, HALF, ROWS], [LACC, RACC],
        [pltpu.VMEM((NZ, NX, 2, 64, E), jnp.bfloat16), CHUNKS[0], pltpu.SMEM((1, SLOTS), jnp.int32),
         pltpu.SemaphoreType.DMA((NX, 2)), pltpu.SemaphoreType.DMA, CHUNKS[1]], any_in=1, any_out=1, limit=FIRST)
    parts = _camp_parts(rows)
    own, other = _sum_load(keep, give)
    keep, give, rows, lam, mu = _call(
        second_kernel, 3, (*slots, own, other, *parts, cap, lim, kept),
        [HALF, HALF, ROWS, LAM, ROWS], [LACC, RACC, LAMB, MUB], CHUNKS, any_in=1, limit=WIDE)
    parts = _camp_parts(rows)
    own, other = _sum_load(keep, give)
    keep, give, both_sums, lam, mu = _call(
        third_kernel, 3, (*slots, own, other, *parts, cap, lim, lam, mu, kept),
        [HALF, HALF, ((2, UB, BLOCK), F32), LAM, ROWS], [LACC, RACC, RACC, LAMB, MUB], CHUNKS, any_in=1, limit=WIDE)
    parts = _camp_parts(both_sums)
    own, other = _sum_load(keep, give)
    duals, user_duals, ratio, value = _call(
        last_kernel, 1, (where, own, other, *parts, cap, lim, lam, mu), [LAM, ROWS, LAM, ROWS])
    return duals.reshape(-1), user_duals.reshape(-1), ratio.reshape(-1), value.reshape(-1)


def solution(mesh):
    fine = Mesh(mesh.devices.reshape(NZ, NX, NCORE, NCAMP), ("z", "x", "core", "camp"))
    users = ("z", "x", "core")
    return jax.shard_map(
        shards,
        mesh=fine,
        in_specs=(P(users, None), P(("camp",) + users, None), P("camp", users), P("camp", users), P("camp"), P(users)),
        out_specs=(P("camp"), P(users), P("camp"), P(users)),
        check_vma=False,
    )
```

```python
import jax
import jax.numpy as jnp
from jax import lax
from jax.experimental import pallas as pl
from jax.experimental.pallas import tpu as pltpu
from jax.sharding import Mesh, PartitionSpec as P

BLOCK = 128
E = 256
SLOTS = 256
UB = 64
CB = 32
NZ, NX, NCORE, NCAMP = 8, 4, 2, 4
UNROLL = 32
GROUP = 32
WIDE = 50
FIRST = 43
AHEAD = 8
F32 = jnp.float32


def _clear(lacc, racc):
    lacc[...] = jnp.zeros_like(lacc)
    racc[...] = jnp.zeros_like(racc)


def _chunk(src, dst, sems, g):
    at = pl.ds(g * GROUP, GROUP)
    return pltpu.make_async_copy(src.at[at], dst.at[at], sems.at[g])


def _each(turns, do):
    def turn(g, carry):
        do(g)
        return carry

    lax.fori_loop(0, turns, turn, 0)


def _fold(x):
    return x.reshape(BLOCK // 8, 8, BLOCK).sum(0)


def _finish_load(lacc, keep, give, core):
    half = CB // 2

    def row(b):
        return jnp.sum(lacc[b].T, axis=0, keepdims=True)

    def turn(b, carry):
        keep[pl.ds(b, 1), :] = row(core * half + b)
        give[pl.ds(b, 1), :] = row((1 - core) * half + b)
        return carry

    lax.fori_loop(0, half, turn, 0, unroll=4)


def _group(ids, cnt, first, size):
    out = []
    for k in range(size):
        slot = first + k
        code = ids[0, slot]
        out.append((slot, code >> 5, code & (CB - 1), slot < cnt))
    return out


def fetch_kernel(users, out, sem):
    copy = pltpu.make_async_copy(users, out, sem)
    copy.start()
    copy.wait()


def first_kernel(core, count, users, part, peer, codes, kept, keep, give, rows, lacc, racc, panel, scores, ids,
                 sems, fetched, stored):
    me = core[0]
    fetch = pltpu.make_async_copy(codes, ids, fetched)
    fetch.start()
    copies = [
        pltpu.make_async_copy(src.at[x], panel.at[:, x, half], sems.at[x, k])
        for x in range(NX)
        for k, (src, half) in enumerate(((part, me), (peer, 1 - me)))
    ]
    for copy in copies:
        copy.start()
    _clear(lacc, racc)
    for copy in copies:
        copy.wait()
    fetch.wait()
    camps = panel.reshape(CB, BLOCK, E)
    cnt = count[0, 0]
    turns = (cnt + GROUP - 1) // GROUP

    def products(g):
        return [
            lax.dot_general(
                camps[cb], users[ub], (((1,), (1,)), ((), ())), preferred_element_type=F32
            ).astype(jnp.bfloat16)
            for _, ub, cb, _ in _group(ids, cnt, g * GROUP, GROUP)
        ]

    def store(g, blocks):
        for k, block in enumerate(blocks):
            scores[g * GROUP + k] = block
        _chunk(scores, kept, stored, g).start()

    def add(g):
        for slot, ub, cb, live in _group(ids, cnt, g * GROUP, GROUP):
            x = jnp.clip(scores[slot].astype(F32), 0.0, 1.0)
            lacc[jnp.where(live, cb, CB)] += x
            racc[jnp.where(live, ub, UB)] += _fold(x)

    store(0, products(0))

    def turn(g, carry):
        blocks = products(g)
        add(g - 1)
        store(g, blocks)
        return carry

    lax.fori_loop(1, turns, turn, 0)
    add(turns - 1)
    _finish_load(lacc, keep, give, core[0])
    rows[...] = racc[:UB].sum(axis=1)
    _each(turns, lambda g: _chunk(scores, kept, stored, g).wait())


def _load_of(own, other, core):
    a, b = own[...], other[...]
    first = core == 0
    return jnp.concatenate([jnp.where(first, a, b), jnp.where(first, b, a)], axis=0)


def _duals(core, own, other, r0, r1, r2, r3, cap_i, lim_i, lam_in, mu_in):
    load = _load_of(own, other, core)
    rows = (r0[...] + r2[...]) + (r1[...] + r3[...])
    cap = cap_i[...].astype(F32)
    lim = lim_i[...].astype(F32)
    lam_new = jnp.maximum(0.0, lam_in + (load - cap) / cap)
    mu_new = jnp.maximum(0.0, mu_in + (rows - lim) / lim)
    return load, cap, lim, lam_new, mu_new


def _round_kernel(core, ids, count, kept, own, other, r0, r1, r2, r3, cap_i, lim_i, lam_in, mu_in,
                  keep, give, rows, values, lam_out, mu_out, lacc, racc, vacc, lamb, mub, scores, loaded):
    cnt = count[0, 0]
    turns = (cnt + GROUP - 1) // GROUP
    _each(jnp.minimum(turns, AHEAD), lambda g: _chunk(kept, scores, loaded, g).start())
    _clear(lacc, racc)
    if vacc is not None:
        vacc[...] = jnp.zeros_like(vacc)
    lam = 0.0 if lam_in is None else lam_in[...]
    mu = 0.0 if mu_in is None else mu_in[...]
    _, _, _, lam_new, mu_new = _duals(core[0], own, other, r0, r1, r2, r3, cap_i, lim_i, lam, mu)
    lam_out[...] = lam_new
    mu_out[...] = mu_new
    lam_bar = 2.0 * lam_new - lam
    mub[:UB] = (2.0 * mu_new - mu)[:, None, :]
    for b in range(CB):
        lamb[b] = jnp.broadcast_to(lam_bar[b:b + 1, :], (BLOCK, BLOCK)).T

    def some(first):
        for slot, ub, cb, live in _group(ids, cnt, first, UNROLL):
            s = scores[slot].astype(F32)
            x = jnp.clip(s - lamb[cb] - mub[ub], 0.0, 1.0)
            lacc[jnp.where(live, cb, CB)] += x
            to_u = jnp.where(live, ub, UB)
            racc[to_u] += _fold(x)
            if vacc is not None:
                vacc[to_u] += _fold(x * s)

    def chunk(g):
        _chunk(kept, scores, loaded, g).wait()

        @pl.when(g + AHEAD < turns)
        def _():
            _chunk(kept, scores, loaded, g + AHEAD).start()

        _each(GROUP // UNROLL, lambda i: some(g * GROUP + i * UNROLL))

    _each(turns, chunk)
    _finish_load(lacc, keep, give, core[0])
    rows[...] = racc[:UB].sum(axis=1)
    if vacc is not None:
        values[...] = vacc[:UB].sum(axis=1)


def second_kernel(core, ids, count, own, other, r0, r1, r2, r3, cap_i, lim_i, kept,
                  keep, give, rows, lam_out, mu_out, lacc, racc, lamb, mub, scores, loaded):
    _round_kernel(core, ids, count, kept, own, other, r0, r1, r2, r3, cap_i, lim_i, None, None,
                  keep, give, rows, None, lam_out, mu_out, lacc, racc, None, lamb, mub, scores, loaded)


def third_kernel(core, ids, count, own, other, r0, r1, r2, r3, cap_i, lim_i, lam_in, mu_in, kept,
                 keep, give, out, lam_out, mu_out, lacc, racc, vacc, lamb, mub, scores, loaded):
    _round_kernel(core, ids, count, kept, own, other, r0, r1, r2, r3, cap_i, lim_i, lam_in, mu_in,
                  keep, give, out.at[0], out.at[1], lam_out, mu_out, lacc, racc, vacc, lamb, mub, scores, loaded)


def last_kernel(core, own, other, p0, p1, p2, p3, cap_i, lim_i, lam_in, mu_in, duals, user_duals, ratio, user_value):
    load, cap, lim, lam_new, mu_new = _duals(
        core[0], own, other, p0.at[0], p1.at[0], p2.at[0], p3.at[0], cap_i, lim_i, lam_in[...], mu_in[...])
    duals[...] = lam_new
    user_duals[...] = mu_new
    ratio[...] = load / cap
    user_value[...] = ((p0[1] + p2[1]) + (p1[1] + p3[1])) / lim


SMEM = pl.BlockSpec(memory_space=pltpu.SMEM)
VMEM = pl.BlockSpec(memory_space=pltpu.VMEM)
ANY = pl.BlockSpec(memory_space=pl.ANY)


def _call(kernel, n_smem, args, outs, scratch=(), more=(), any_in=0, any_out=0, limit=20):
    return pl.pallas_call(
        kernel,
        in_specs=[SMEM] * n_smem + [VMEM] * (len(args) - n_smem - any_in) + [ANY] * any_in,
        out_specs=[ANY] * any_out + [VMEM] * (len(outs) - any_out),
        out_shape=[jax.ShapeDtypeStruct(s, d) for s, d in outs],
        scratch_shapes=[pltpu.VMEM(s, F32) for s in scratch] + list(more),
        compiler_params=pltpu.CompilerParams(vmem_limit_bytes=limit * 2 ** 20),
    )(*args)


LACC = (CB + 1, BLOCK, BLOCK)
RACC = (UB + 1, 8, BLOCK)
HALF = ((CB // 2, BLOCK), F32)
ROWS = ((UB, BLOCK), F32)
LAM = ((CB, BLOCK), F32)
MUB = (UB, 1, BLOCK)
SCORES = ((SLOTS, BLOCK, BLOCK), jnp.bfloat16)
CHUNKS = [pltpu.VMEM(*SCORES), pltpu.SemaphoreType.DMA((SLOTS // GROUP,))]
LAMB = (CB, BLOCK, BLOCK)


def _spread(x, axes, n):
    return lax.all_to_all(jnp.broadcast_to(x[None], (n,) + x.shape), axes, 0, 0, tiled=True)


def _swap(x):
    return lax.ppermute(x, "core", [(0, 1), (1, 0)])


def spread_kernel(keep, got, out):
    out[...] = jnp.broadcast_to((keep[...] + got[...])[None], out.shape)


def sum_kernel(parts, out):
    out[...] = parts[...].sum(0)


def _sum_load(keep, give):
    (wide,) = _call(spread_kernel, 0, (keep, _swap(give)), [((NZ * NX,) + HALF[0], F32)])
    wide = lax.all_to_all(wide, ("z", "x"), 0, 0, tiled=True)
    (own,) = _call(sum_kernel, 0, (wide,), [HALF])
    return own, _swap(own)


def _shift(x, k):
    return lax.ppermute(x, "camp", [((i + k) % NCAMP, i) for i in range(NCAMP)])


def _camp_parts(x):
    return x, _shift(x, 1), _shift(x, 2), _shift(x, 3)


def shards(user_emb, camp_emb, block_ids, block_count, capacity, user_limit):
    where = jnp.reshape(lax.axis_index("core"), (1,)).astype(jnp.int32)
    camp_emb, where = lax.optimization_barrier((camp_emb, where))
    cap = capacity.reshape(CB, BLOCK)
    lim = user_limit.reshape(UB, BLOCK)
    users = user_emb.reshape(UB, BLOCK, E)

    part = _spread(camp_emb, "z", NZ)
    part = _spread(part.reshape(NZ, 64, E), "x", NX).reshape(NX, NZ, 64, E)
    part, users = lax.optimization_barrier((part, users))
    (users,) = _call(
        fetch_kernel, 0, (users,), [(users.shape, users.dtype)], [], [pltpu.SemaphoreType.DMA], any_in=1, limit=4)
    peer = _swap(part)

    slots = (where, block_ids, block_count)
    kept, keep, give, rows = _call(
        first_kernel, 2, (where, block_count, users, part, peer, block_ids), [SCORES, HALF, HALF, ROWS], [LACC, RACC],
        [pltpu.VMEM((NZ, NX, 2, 64, E), jnp.bfloat16), CHUNKS[0], pltpu.SMEM((1, SLOTS), jnp.int32),
         pltpu.SemaphoreType.DMA((NX, 2)), pltpu.SemaphoreType.DMA, CHUNKS[1]], any_in=1, any_out=1, limit=FIRST)
    parts = _camp_parts(rows)
    own, other = _sum_load(keep, give)
    keep, give, rows, lam, mu = _call(
        second_kernel, 3, (*slots, own, other, *parts, cap, lim, kept),
        [HALF, HALF, ROWS, LAM, ROWS], [LACC, RACC, LAMB, MUB], CHUNKS, any_in=1, limit=WIDE)
    parts = _camp_parts(rows)
    own, other = _sum_load(keep, give)
    keep, give, both_sums, lam, mu = _call(
        third_kernel, 3, (*slots, own, other, *parts, cap, lim, lam, mu, kept),
        [HALF, HALF, ((2, UB, BLOCK), F32), LAM, ROWS], [LACC, RACC, RACC, LAMB, MUB], CHUNKS, any_in=1, limit=WIDE)
    parts = _camp_parts(both_sums)
    own, other = _sum_load(keep, give)
    duals, user_duals, ratio, value = _call(
        last_kernel, 1, (where, own, other, *parts, cap, lim, lam, mu), [LAM, ROWS, LAM, ROWS])
    return duals.reshape(-1), user_duals.reshape(-1), ratio.reshape(-1), value.reshape(-1)


def solution(mesh):
    fine = Mesh(mesh.devices.reshape(NZ, NX, NCORE, NCAMP), ("z", "x", "core", "camp"))
    users = ("z", "x", "core")
    return jax.shard_map(
        shards,
        mesh=fine,
        in_specs=(P(users, None), P(("camp",) + users, None), P("camp", users), P("camp", users), P("camp"), P(users)),
        out_specs=(P("camp"), P(users), P("camp"), P(users)),
        check_vma=False,
    )
```

```python
import jax
import jax.numpy as jnp
from jax import lax
from jax.experimental import pallas as pl
from jax.experimental.pallas import tpu as pltpu
from jax.sharding import Mesh, PartitionSpec as P

BLOCK = 128
PART = 64
E = 256
SLOTS = 256
UB = 64
UB2 = 128
CB = 32
NZ, NX, NCORE, NCAMP = 8, 4, 2, 4
GROUP = 32
STEP = 32
CHUNKS = SLOTS // GROUP
WIDE = 50
FIRST = 50
F32 = jnp.float32


def _each(turns, do):
    def turn(g, carry):
        do(g)
        return carry

    lax.fori_loop(0, turns, turn, 0)


def _clear(*accs):
    for acc in accs:
        if acc is not None:
            acc[...] = jnp.zeros_like(acc)


def _chunk(src, dst, sems, g):
    at = pl.ds(g * GROUP, GROUP)
    return pltpu.make_async_copy(src.at[at], dst.at[at], sems.at[g])


def _fold(x):
    return x.reshape(PART // 8, 8, BLOCK).sum(0)


def _finish_load(lacc, out):
    def turn(r, carry):
        both = lacc[pl.ds(2 * r, 2)].reshape(BLOCK, BLOCK)
        out[pl.ds(r, 1), :] = jnp.sum(both.T, axis=0, keepdims=True)
        return carry

    lax.fori_loop(0, CB // 2, turn, 0, unroll=4)


def _turns(cnt):
    return (cnt + GROUP - 1) // GROUP


def _group(ids, cnt, first, size):
    out = []
    for k in range(size):
        slot = first + k
        code = ids[0, slot]
        out.append((slot, code >> 5, code & (CB - 1), slot < cnt))
    return out


def first_kernel(count0, count1, part, codes0, codes1, from0, from1, kept, load, rows, lacc, racc, scores, ids0, ids1,
                 users0, users1, fetched, stored):
    fetches = [
        pltpu.make_async_copy(src, dst, fetched.at[k])
        for k, (src, dst) in enumerate(((codes0, ids0), (from0, users0), (codes1, ids1), (from1, users1)))
    ]
    for fetch in fetches:
        fetch.start()
    _clear(lacc, racc)

    for which, (ids, count, users) in enumerate(((ids0, count0, users0), (ids1, count1, users1))):
        cnt = count[0, 0]
        turns = _turns(cnt)
        base = which * SLOTS
        fetches[2 * which].wait()
        fetches[2 * which + 1].wait()

        def products(g, ids=ids, cnt=cnt, users=users):
            return [
                lax.dot_general(
                    part[cb & (NX - 1), cb >> 2], users[ub], (((1,), (1,)), ((), ())), preferred_element_type=F32
                ).astype(jnp.bfloat16)
                for _, ub, cb, _ in _group(ids, cnt, g * GROUP, GROUP)
            ]

        def store(g, blocks, which=which, base=base):
            for k, block in enumerate(blocks):
                scores[base + g * GROUP + k] = block
            _chunk(scores, kept, stored, which * CHUNKS + g).start()

        def add(g, ids=ids, cnt=cnt, which=which, base=base):
            for slot, ub, cb, live in _group(ids, cnt, g * GROUP, GROUP):
                x = jnp.clip(scores[base + slot].astype(F32), 0.0, 1.0)
                lacc[jnp.where(live, cb, CB)] += x
                racc[jnp.where(live, ub + which * UB, UB2)] += _fold(x)

        store(0, products(0))

        def turn(g, carry, products=products, add=add, store=store):
            blocks = products(g)
            add(g - 1)
            store(g, blocks)
            return carry

        lax.fori_loop(1, turns, turn, 0)
        add(turns - 1)

    _finish_load(lacc, load)
    rows[...] = racc[:UB2].sum(axis=1)
    for which, count in enumerate((count0, count1)):
        _each(_turns(count[0, 0]), lambda g, w=which: _chunk(scores, kept, stored, w * CHUNKS + g).wait())


def _duals(load_in, r0, r1, r2, r3, cap_i, lim_i, lam_in, mu_in):
    load = load_in[...]
    rows = (r0[...] + r2[...]) + (r1[...] + r3[...])
    cap = cap_i[...].astype(F32)
    lim = lim_i[...].astype(F32)
    lam_new = jnp.maximum(0.0, lam_in + (load - cap) / cap)
    mu_new = jnp.maximum(0.0, mu_in + (rows - lim) / lim)
    return load, cap, lim, lam_new, mu_new


def _round_kernel(id0, id1, count0, count1, load_in, r0, r1, r2, r3, cap_i, lim_i, lam_in, mu_in, kept,
                  load, rows, values, lam_out, mu_out, lacc, racc, vacc, lamb, mub, scores, loaded):
    lists = ((id0, count0[0, 0]), (id1, count1[0, 0]))
    for which, (_, cnt) in enumerate(lists):
        _each(_turns(cnt), lambda g, w=which: _chunk(kept, scores, loaded, w * CHUNKS + g).start())
    _clear(lacc, racc, vacc)
    lam = 0.0 if lam_in is None else lam_in[...]
    mu = 0.0 if mu_in is None else mu_in[...]
    _, _, _, lam_new, mu_new = _duals(load_in, r0, r1, r2, r3, cap_i, lim_i, lam, mu)
    lam_out[...] = lam_new
    mu_out[...] = mu_new
    lam_bar = 2.0 * lam_new - lam
    mub[:UB2] = (2.0 * mu_new - mu)[:, None, :]
    for r in range(CB // 2):
        tall = jnp.broadcast_to(lam_bar[r:r + 1, :], (BLOCK, BLOCK)).T
        lamb[2 * r] = tall[:PART]
        lamb[2 * r + 1] = tall[PART:]

    for which, (ids, cnt) in enumerate(lists):

        def some(first, ids=ids, cnt=cnt, which=which):
            for slot, ub, cb, live in _group(ids, cnt, first, STEP):
                s = scores[which * SLOTS + slot].astype(F32)
                x = jnp.clip(s - lamb[cb] - mub[ub + which * UB], 0.0, 1.0)
                lacc[jnp.where(live, cb, CB)] += x
                to_u = jnp.where(live, ub + which * UB, UB2)
                racc[to_u] += _fold(x)
                if vacc is not None:
                    vacc[to_u] += _fold(x * s)

        def chunk(g, which=which, some=some):
            _chunk(kept, scores, loaded, which * CHUNKS + g).wait()
            _each(GROUP // STEP, lambda i: some(g * GROUP + i * STEP))

        _each(_turns(cnt), chunk)

    _finish_load(lacc, load)
    rows[...] = racc[:UB2].sum(axis=1)
    if vacc is not None:
        values[...] = vacc[:UB2].sum(axis=1)


def second_kernel(id0, id1, count0, count1, load_in, r0, r1, r2, r3, cap_i, lim_i, kept,
                  load, rows, lam_out, mu_out, lacc, racc, lamb, mub, scores, loaded):
    _round_kernel(id0, id1, count0, count1, load_in, r0, r1, r2, r3, cap_i, lim_i, None, None, kept,
                  load, rows, None, lam_out, mu_out, lacc, racc, None, lamb, mub, scores, loaded)


def third_kernel(id0, id1, count0, count1, load_in, r0, r1, r2, r3, cap_i, lim_i, lam_in, mu_in, kept,
                 load, out, lam_out, mu_out, lacc, racc, vacc, lamb, mub, scores, loaded):
    _round_kernel(id0, id1, count0, count1, load_in, r0, r1, r2, r3, cap_i, lim_i, lam_in, mu_in, kept,
                  load, out.at[0], out.at[1], lam_out, mu_out, lacc, racc, vacc, lamb, mub, scores, loaded)


def users_kernel(p0, p1, p2, p3, lim_i, mu_in, user_duals, user_value):
    mine = pl.ds(0, UB)
    rows, value = ((p0[k, mine] + p2[k, mine]) + (p1[k, mine] + p3[k, mine]) for k in range(2))
    lim = lim_i[mine].astype(F32)
    user_duals[...] = jnp.maximum(0.0, mu_in[mine] + (rows - lim) / lim)
    user_value[...] = value / lim


def campaigns_kernel(parts, cap_i, lam_in, out):
    load = parts[...].sum(0)
    cap = cap_i[...].astype(F32)
    out[0] = jnp.maximum(0.0, lam_in[...] + (load - cap) / cap)
    out[1] = load / cap


def spread_kernel(load, out):
    out[...] = jnp.broadcast_to(load[...][None], out.shape)


def sum_kernel(parts, out):
    out[...] = parts[...].sum(0)


def pair_kernel(mine, theirs, out):
    half = pl.ds(0, UB)
    rest = pl.ds(UB, UB)
    out[..., half, :] = mine[..., half, :] + theirs[..., rest, :]
    out[..., rest, :] = mine[..., rest, :] + theirs[..., half, :]


SMEM = pl.BlockSpec(memory_space=pltpu.SMEM)
VMEM = pl.BlockSpec(memory_space=pltpu.VMEM)
ANY = pl.BlockSpec(memory_space=pl.ANY)


def _call(kernel, n_smem, args, outs, scratch=(), more=(), any_in=0, any_out=0, limit=4):
    return pl.pallas_call(
        kernel,
        in_specs=[SMEM] * n_smem + [VMEM] * (len(args) - n_smem - any_in) + [ANY] * any_in,
        out_specs=[ANY] * any_out + [VMEM] * (len(outs) - any_out),
        out_shape=[jax.ShapeDtypeStruct(s, d) for s, d in outs],
        scratch_shapes=[pltpu.VMEM(s, F32) for s in scratch] + list(more),
        compiler_params=pltpu.CompilerParams(vmem_limit_bytes=limit * 2 ** 20),
    )(*args)


LACC = (CB + 1, PART, BLOCK)
RACC = (UB2 + 1, 8, BLOCK)
LOAD = ((CB // 2, BLOCK), F32)
ROWS = ((UB2, BLOCK), F32)
MUB = (UB2, 1, BLOCK)
LAMB = (CB, PART, BLOCK)
SCORES = ((2 * SLOTS, PART, BLOCK), jnp.bfloat16)
KEPT = [pltpu.VMEM(*SCORES), pltpu.SemaphoreType.DMA((2 * CHUNKS,))]


def _spread(x, axes, n):
    return lax.all_to_all(jnp.broadcast_to(x[None], (n,) + x.shape), axes, 0, 0, tiled=True)


def _swap(x):
    return lax.ppermute(x, "core", [(0, 1), (1, 0)])


def _load_parts(load):
    (wide,) = _call(spread_kernel, 0, (load,), [((NZ * NX,) + LOAD[0], F32)])
    return lax.all_to_all(wide, ("z", "x"), 0, 0, tiled=True)


def _shift(x, k):
    return lax.ppermute(x, "camp", [((i + k) % NCAMP, i) for i in range(NCAMP)])


def _camp_parts(x):
    (x,) = _call(pair_kernel, 0, (x, _swap(x)), [(x.shape, F32)])
    return x, _shift(x, 1), _shift(x, 2), _shift(x, 3)


def shards(user_emb, camp_emb, block_ids, block_count, capacity, user_limit):
    core = lax.axis_index("core")
    camp_emb, core = lax.optimization_barrier((camp_emb, core))
    users = user_emb.reshape(UB, BLOCK, E)
    users1 = _swap(users)
    ids1 = _swap(block_ids)
    count1 = _swap(block_count)
    lim1 = _swap(user_limit)

    part = _spread(camp_emb, "z", NZ)
    part = _spread(part.reshape(NZ, PART, E), "x", NX).reshape(NX, NZ, PART, E)

    kept, load, rows = _call(
        first_kernel, 2, (block_count, count1, part, block_ids, ids1, users, users1), [SCORES, LOAD, ROWS],
        [LACC, RACC],
        [KEPT[0], pltpu.SMEM((1, SLOTS), jnp.int32), pltpu.SMEM((1, SLOTS), jnp.int32),
         pltpu.VMEM((UB, BLOCK, E), jnp.bfloat16), pltpu.VMEM((UB, BLOCK, E), jnp.bfloat16),
         pltpu.SemaphoreType.DMA((4,)), KEPT[1]], any_in=4, any_out=1, limit=FIRST)
    halves = capacity.reshape(CB // 2, 2, 2, PART)
    cap = jnp.where(core == 0, halves[:, :, 0], halves[:, :, 1]).reshape(CB // 2, BLOCK)
    lim = jnp.concatenate([user_limit, lim1]).reshape(UB2, BLOCK)
    lists = (block_ids, ids1, block_count, count1)

    parts = _camp_parts(rows)
    (load,) = _call(sum_kernel, 0, (_load_parts(load),), [LOAD])
    load, rows, lam, mu = _call(
        second_kernel, 4, (*lists, load, *parts, cap, lim, kept),
        [LOAD, ROWS, LOAD, ROWS], [LACC, RACC, LAMB, MUB], KEPT, any_in=1, limit=WIDE)
    parts = _camp_parts(rows)
    (load,) = _call(sum_kernel, 0, (_load_parts(load),), [LOAD])
    load, sums, lam, mu = _call(
        third_kernel, 4, (*lists, load, *parts, cap, lim, lam, mu, kept),
        [LOAD, ((2, UB2, BLOCK), F32), LOAD, ROWS], [LACC, RACC, RACC, LAMB, MUB], KEPT, any_in=1, limit=WIDE)
    parts = _camp_parts(sums)
    (pair,) = _call(campaigns_kernel, 0, (_load_parts(load), cap, lam), [((2, CB // 2, BLOCK), F32)])
    user_duals, value = _call(users_kernel, 0, (*parts, lim, mu), [((UB, BLOCK), F32)] * 2)
    other = _swap(pair)
    first = core == 0
    both = jnp.stack([jnp.where(first, pair, other), jnp.where(first, other, pair)])
    both = both.reshape(2, 2, CB, PART).transpose(1, 2, 0, 3).reshape(2, CB * BLOCK)
    return both[0], user_duals.reshape(-1), both[1], value.reshape(-1)


def solution(mesh):
    fine = Mesh(mesh.devices.reshape(NZ, NX, NCORE, NCAMP), ("z", "x", "core", "camp"))
    users = ("z", "x", "core")
    return jax.shard_map(
        shards,
        mesh=fine,
        in_specs=(P(users, None), P(("camp",) + users, None), P("camp", users), P("camp", users), P("camp"), P(users)),
        out_specs=(P("camp"), P(users), P("camp"), P(users)),
        check_vma=False,
    )
```

```python
import jax
import jax.numpy as jnp
from jax import lax
from jax.experimental import pallas as pl
from jax.experimental.pallas import tpu as pltpu
from jax.sharding import Mesh, PartitionSpec as P

BLOCK = 128
PART = 64
E = 256
SLOTS = 256
UB = 64
UB2 = 128
CB = 32
NZ, NX, NCORE, NCAMP = 8, 4, 2, 4
GROUP = 32
STEP = 32
CHUNKS = SLOTS // GROUP
WIDE = 50
FIRST = 43
F32 = jnp.float32


def _each(turns, do):
    def turn(g, carry):
        do(g)
        return carry

    lax.fori_loop(0, turns, turn, 0)


def _clear(*accs):
    for acc in accs:
        if acc is not None:
            acc[...] = jnp.zeros_like(acc)


def _load(kept, scores, sems, which, g):
    to = pl.ds(which * SLOTS + g * GROUP, GROUP)
    return pltpu.make_async_copy(kept.at[pl.ds(g * GROUP, GROUP)], scores.at[to], sems.at[which * CHUNKS + g])


def _save(scores, kept, sems, which, g):
    at = pl.ds(g * GROUP, GROUP)
    return pltpu.make_async_copy(scores.at[at, pl.ds(which * PART, PART)], kept.at[at], sems.at[which, g])


def _fold(x):
    return x.reshape(x.shape[0] // 8, 8, BLOCK).sum(0)


def _finish_load(lacc, out):
    def turn(r, carry):
        both = lacc[pl.ds(2 * r, 2)].reshape(BLOCK, BLOCK)
        out[pl.ds(r, 1), :] = jnp.sum(both.T, axis=0, keepdims=True)
        return carry

    lax.fori_loop(0, CB // 2, turn, 0, unroll=4)


def _turns(cnt):
    return (cnt + GROUP - 1) // GROUP


def _group(ids, cnt, first, size):
    out = []
    for k in range(size):
        slot = first + k
        code = ids[0, slot]
        out.append((slot, code >> 5, code & (CB - 1), slot < cnt))
    return out


def fetch_kernel(users, out, sem):
    copy = pltpu.make_async_copy(users, out, sem)
    copy.start()
    copy.wait()


def first_kernel(count, users, part, peer, codes, kept0, kept1, keep, give, rows, lacc, racc, panel, scores, ids,
                 sems, fetched, stored):
    fetch = pltpu.make_async_copy(codes, ids, fetched)
    fetch.start()
    copies = [
        pltpu.make_async_copy(src.at[x], panel.at[:, x, half], sems.at[x, half])
        for x in range(NX)
        for half, src in enumerate((part, peer))
    ]
    for copy in copies:
        copy.start()
    _clear(lacc, racc)
    for copy in copies:
        copy.wait()
    fetch.wait()
    camps = panel.reshape(CB, BLOCK, E)
    cnt = count[0, 0]
    turns = _turns(cnt)
    kepts = (kept0, kept1)

    def products(g):
        return [
            lax.dot_general(
                camps[cb], users[ub], (((1,), (1,)), ((), ())), preferred_element_type=F32
            ).astype(jnp.bfloat16)
            for _, ub, cb, _ in _group(ids, cnt, g * GROUP, GROUP)
        ]

    def store(g, blocks):
        for k, block in enumerate(blocks):
            scores[g * GROUP + k] = block
        for which, kept in enumerate(kepts):
            _save(scores, kept, stored, which, g).start()

    def add(g):
        for slot, ub, cb, live in _group(ids, cnt, g * GROUP, GROUP):
            x = jnp.clip(scores[slot].astype(F32), 0.0, 1.0)
            lacc[jnp.where(live, cb, CB)] += x
            racc[jnp.where(live, ub, UB)] += _fold(x)

    store(0, products(0))

    def turn(g, carry):
        blocks = products(g)
        add(g - 1)
        store(g, blocks)
        return carry

    lax.fori_loop(1, turns, turn, 0)
    add(turns - 1)

    def finish(r, carry):
        pair = lacc[pl.ds(2 * r, 2)]
        for which, out in enumerate((keep, give)):
            both = pair[:, which * PART:(which + 1) * PART].reshape(BLOCK, BLOCK)
            out[pl.ds(r, 1), :] = jnp.sum(both.T, axis=0, keepdims=True)
        return carry

    lax.fori_loop(0, CB // 2, finish, 0, unroll=2)
    rows[...] = racc[:UB].sum(axis=1)
    for which, kept in enumerate(kepts):
        _each(turns, lambda g, w=which, k=kept: _save(scores, k, stored, w, g).wait())


def _duals(load_in, r0, r1, r2, r3, cap_i, lim_i, lam_in, mu_in):
    load = load_in[...]
    rows = (r0[...] + r2[...]) + (r1[...] + r3[...])
    cap = cap_i[...].astype(F32)
    lim = lim_i[...].astype(F32)
    lam_new = jnp.maximum(0.0, lam_in + (load - cap) / cap)
    mu_new = jnp.maximum(0.0, mu_in + (rows - lim) / lim)
    return load, cap, lim, lam_new, mu_new


def _round_kernel(id0, id1, count0, count1, load_in, r0, r1, r2, r3, cap_i, lim_i, lam_in, mu_in, kepts,
                  load, rows, values, lam_out, mu_out, lacc, racc, vacc, lamb, mub, scores, loaded):
    lists = ((id0, count0[0, 0]), (id1, count1[0, 0]))
    for which, (_, cnt) in enumerate(lists):
        _each(_turns(cnt), lambda g, w=which: _load(kepts[w], scores, loaded, w, g).start())
    _clear(lacc, racc, vacc)
    lam = 0.0 if lam_in is None else lam_in[...]
    mu = 0.0 if mu_in is None else mu_in[...]
    _, _, _, lam_new, mu_new = _duals(load_in, r0, r1, r2, r3, cap_i, lim_i, lam, mu)
    lam_out[...] = lam_new
    mu_out[...] = mu_new
    lam_bar = 2.0 * lam_new - lam
    mub[:UB2] = (2.0 * mu_new - mu)[:, None, :]
    for r in range(CB // 2):
        tall = jnp.broadcast_to(lam_bar[r:r + 1, :], (BLOCK, BLOCK)).T
        lamb[2 * r] = tall[:PART]
        lamb[2 * r + 1] = tall[PART:]

    for which, (ids, cnt) in enumerate(lists):

        def some(first, ids=ids, cnt=cnt, which=which):
            for slot, ub, cb, live in _group(ids, cnt, first, STEP):
                s = scores[which * SLOTS + slot].astype(F32)
                x = jnp.clip(s - lamb[cb] - mub[ub + which * UB], 0.0, 1.0)
                lacc[jnp.where(live, cb, CB)] += x
                to_u = jnp.where(live, ub + which * UB, UB2)
                racc[to_u] += _fold(x)
                if vacc is not None:
                    vacc[to_u] += _fold(x * s)

        def chunk(g, which=which, some=some):
            _load(kepts[which], scores, loaded, which, g).wait()
            _each(GROUP // STEP, lambda i: some(g * GROUP + i * STEP))

        _each(_turns(cnt), chunk)

    _finish_load(lacc, load)
    rows[...] = racc[:UB2].sum(axis=1)
    if vacc is not None:
        values[...] = vacc[:UB2].sum(axis=1)


def second_kernel(id0, id1, count0, count1, load_in, r0, r1, r2, r3, cap_i, lim_i, kept0, kept1,
                  load, rows, lam_out, mu_out, lacc, racc, lamb, mub, scores, loaded):
    _round_kernel(id0, id1, count0, count1, load_in, r0, r1, r2, r3, cap_i, lim_i, None, None, (kept0, kept1),
                  load, rows, None, lam_out, mu_out, lacc, racc, None, lamb, mub, scores, loaded)


def third_kernel(id0, id1, count0, count1, load_in, r0, r1, r2, r3, cap_i, lim_i, lam_in, mu_in, kept0, kept1,
                 load, out, lam_out, mu_out, lacc, racc, vacc, lamb, mub, scores, loaded):
    _round_kernel(id0, id1, count0, count1, load_in, r0, r1, r2, r3, cap_i, lim_i, lam_in, mu_in, (kept0, kept1),
                  load, out.at[0], out.at[1], lam_out, mu_out, lacc, racc, vacc, lamb, mub, scores, loaded)


def last_kernel(core, p0, p1, p2, p3, lim_i, mu_in, mine, theirs, duals, user_duals, ratio, user_value):
    half = pl.ds(0, UB)
    rows, value = ((p0[k, half] + p2[k, half]) + (p1[k, half] + p3[k, half]) for k in range(2))
    lim = lim_i[half].astype(F32)
    user_duals[...] = jnp.maximum(0.0, mu_in[half] + (rows - lim) / lim)
    user_value[...] = value / lim
    first = core[0] == 0
    for k, out in enumerate((duals, ratio)):
        a, b = jnp.where(first, mine[k], theirs[k]), jnp.where(first, theirs[k], mine[k])
        even = jnp.concatenate([a[:, :PART], b[:, :PART]], axis=1)
        odd = jnp.concatenate([a[:, PART:], b[:, PART:]], axis=1)
        for r in range(CB // 2):
            out[2 * r:2 * r + 1, :] = even[r:r + 1]
            out[2 * r + 1:2 * r + 2, :] = odd[r:r + 1]


def campaigns_kernel(parts, cap_i, lam_in, out):
    load = parts[...].sum(0)
    cap = cap_i[...].astype(F32)
    out[0] = jnp.maximum(0.0, lam_in[...] + (load - cap) / cap)
    out[1] = load / cap


def spread_kernel(load, out):
    out[...] = jnp.broadcast_to(load[...][None], out.shape)


def spread_sum_kernel(keep, got, out):
    out[...] = jnp.broadcast_to((keep[...] + got[...])[None], out.shape)


def join_kernel(mine, theirs, out):
    out[:UB] = mine[...]
    out[UB:] = theirs[...]


def sum_kernel(parts, out):
    out[...] = parts[...].sum(0)


def pair_kernel(mine, theirs, out):
    half = pl.ds(0, UB)
    rest = pl.ds(UB, UB)
    out[..., half, :] = mine[..., half, :] + theirs[..., rest, :]
    out[..., rest, :] = mine[..., rest, :] + theirs[..., half, :]


SMEM = pl.BlockSpec(memory_space=pltpu.SMEM)
VMEM = pl.BlockSpec(memory_space=pltpu.VMEM)
ANY = pl.BlockSpec(memory_space=pl.ANY)


def _call(kernel, n_smem, args, outs, scratch=(), more=(), any_in=0, any_out=0, limit=4):
    return pl.pallas_call(
        kernel,
        in_specs=[SMEM] * n_smem + [VMEM] * (len(args) - n_smem - any_in) + [ANY] * any_in,
        out_specs=[ANY] * any_out + [VMEM] * (len(outs) - any_out),
        out_shape=[jax.ShapeDtypeStruct(s, d) for s, d in outs],
        scratch_shapes=[pltpu.VMEM(s, F32) for s in scratch] + list(more),
        compiler_params=pltpu.CompilerParams(vmem_limit_bytes=limit * 2 ** 20),
    )(*args)


LACC = (CB + 1, PART, BLOCK)
LACC1 = (CB + 1, BLOCK, BLOCK)
RACC1 = (UB + 1, 8, BLOCK)
RACC = (UB2 + 1, 8, BLOCK)
LOAD = ((CB // 2, BLOCK), F32)
ROWS = ((UB2, BLOCK), F32)
MUB = (UB2, 1, BLOCK)
LAMB = (CB, PART, BLOCK)
SCORES = ((SLOTS, PART, BLOCK), jnp.bfloat16)
ROOMY = ((2 * SLOTS, PART, BLOCK), jnp.bfloat16)
KEPT = [pltpu.VMEM((2 * SLOTS, PART, BLOCK), jnp.bfloat16), pltpu.SemaphoreType.DMA((2 * CHUNKS,))]


def _spread(x, axes, n):
    return lax.all_to_all(jnp.broadcast_to(x[None], (n,) + x.shape), axes, 0, 0, tiled=True)


def _swap(x):
    return lax.ppermute(x, "core", [(0, 1), (1, 0)])


def _load_parts(load):
    (wide,) = _call(spread_kernel, 0, (load,), [((NZ * NX,) + LOAD[0], F32)])
    return lax.all_to_all(wide, ("z", "x"), 0, 0, tiled=True)


def _shift(x, k):
    return lax.ppermute(x, "camp", [((i + k) % NCAMP, i) for i in range(NCAMP)])


def _camp_parts(x, kernel, shape):
    (x,) = _call(kernel, 0, (x, _swap(x)), [(shape, F32)])
    return x, _shift(x, 1), _shift(x, 2), _shift(x, 3)


def shards(user_emb, camp_emb, block_ids, block_count, capacity, user_limit):
    where = jnp.reshape(lax.axis_index("core"), (1,)).astype(jnp.int32)
    camp_emb, where = lax.optimization_barrier((camp_emb, where))
    users = user_emb.reshape(UB, BLOCK, E)

    part = _spread(camp_emb, "z", NZ)
    part = _spread(part.reshape(NZ, PART, E), "x", NX).reshape(NX, NZ, PART, E)
    part, users = lax.optimization_barrier((part, users))
    (users,) = _call(
        fetch_kernel, 0, (users,), [(users.shape, users.dtype)], [], [pltpu.SemaphoreType.DMA], any_in=1)
    peer = _swap(part)

    kept0, give1, keep, give, rows = _call(
        first_kernel, 1, (block_count, users, part, peer, block_ids), [ROOMY, SCORES, LOAD, LOAD, ((UB, BLOCK), F32)],
        [LACC1, RACC1],
        [pltpu.VMEM((NZ, NX, 2, PART, E), jnp.bfloat16), pltpu.VMEM((SLOTS, BLOCK, BLOCK), jnp.bfloat16),
         pltpu.SMEM((1, SLOTS), jnp.int32), pltpu.SemaphoreType.DMA((NX, 2)), pltpu.SemaphoreType.DMA,
         pltpu.SemaphoreType.DMA((2, CHUNKS))], any_in=1, any_out=2, limit=FIRST)
    (wide,) = _call(spread_sum_kernel, 0, (keep, _swap(give)), [((NZ * NX,) + LOAD[0], F32)])
    wide, rows, give1, block_ids, block_count, user_limit, capacity = lax.optimization_barrier(
        (wide, rows, give1, block_ids, block_count, user_limit, capacity))
    wide = lax.all_to_all(wide, ("z", "x"), 0, 0, tiled=True)
    parts = _camp_parts(rows, join_kernel, ROWS[0])
    kept1 = _swap(give1)
    ids1, count1, lim1 = _swap(block_ids), _swap(block_count), _swap(user_limit)
    halves = capacity.reshape(CB // 2, 2, 2, PART)
    cap = jnp.where(where[0] == 0, halves[:, :, 0], halves[:, :, 1]).reshape(CB // 2, BLOCK)
    lim = jnp.concatenate([user_limit, lim1]).reshape(UB2, BLOCK)
    lists = (block_ids, ids1, block_count, count1)
    (load,) = _call(sum_kernel, 0, (wide,), [LOAD])

    load, rows, lam, mu = _call(
        second_kernel, 4, (*lists, load, *parts, cap, lim, kept0, kept1),
        [LOAD, ROWS, LOAD, ROWS], [LACC, RACC, LAMB, MUB], KEPT, any_in=2, limit=WIDE)
    parts = _camp_parts(rows, pair_kernel, ROWS[0])
    (load,) = _call(sum_kernel, 0, (_load_parts(load),), [LOAD])
    load, sums, lam, mu = _call(
        third_kernel, 4, (*lists, load, *parts, cap, lim, lam, mu, kept0, kept1),
        [LOAD, ((2, UB2, BLOCK), F32), LOAD, ROWS], [LACC, RACC, RACC, LAMB, MUB], KEPT, any_in=2, limit=WIDE)
    parts = _camp_parts(sums, pair_kernel, (2,) + ROWS[0])
    (pair,) = _call(campaigns_kernel, 0, (_load_parts(load), cap, lam), [((2, CB // 2, BLOCK), F32)])
    duals, user_duals, ratio, value = _call(
        last_kernel, 1, (where, *parts, lim, mu, pair, _swap(pair)),
        [((CB, BLOCK), F32), ((UB, BLOCK), F32)] * 2)
    return duals.reshape(-1), user_duals.reshape(-1), ratio.reshape(-1), value.reshape(-1)


def solution(mesh):
    fine = Mesh(mesh.devices.reshape(NZ, NX, NCORE, NCAMP), ("z", "x", "core", "camp"))
    users = ("z", "x", "core")
    return jax.shard_map(
        shards,
        mesh=fine,
        in_specs=(P(users, None), P(("camp",) + users, None), P("camp", users), P("camp", users), P("camp"), P(users)),
        out_specs=(P("camp"), P(users), P("camp"), P(users)),
        check_vma=False,
    )
```

```python
import jax
import jax.numpy as jnp
from jax import lax
from jax.experimental import pallas as pl
from jax.experimental.pallas import tpu as pltpu
from jax.sharding import Mesh, PartitionSpec as P

BLOCK = 128
PART = 64
E = 256
SLOTS = 256
UB = 64
UB2 = 128
CB = 32
NZ, NX, NCORE, NCAMP = 8, 4, 2, 4
GROUP = 32
STEP = 32
CHUNKS = SLOTS // GROUP
WIDE = 50
FIRST = 43
F32 = jnp.float32


def _each(turns, do):
    def turn(g, carry):
        do(g)
        return carry

    lax.fori_loop(0, turns, turn, 0)


def _clear(*accs):
    for acc in accs:
        if acc is not None:
            acc[...] = jnp.zeros_like(acc)


def _load(kept, scores, sems, which, g):
    to = pl.ds(which * SLOTS + g * GROUP, GROUP)
    return pltpu.make_async_copy(kept.at[pl.ds(g * GROUP, GROUP)], scores.at[to], sems.at[which * CHUNKS + g])


def _save(scores, kept, sems, which, g):
    at = pl.ds(g * GROUP, GROUP)
    return pltpu.make_async_copy(scores.at[at, pl.ds(which * PART, PART)], kept.at[at], sems.at[which, g])


def _fold(x):
    return x.reshape(x.shape[0] // 8, 8, BLOCK).sum(0)


def _finish_load(lacc, out):
    def turn(r, carry):
        both = lacc[pl.ds(2 * r, 2)].reshape(BLOCK, BLOCK)
        out[pl.ds(r, 1), :] = jnp.sum(both.T, axis=0, keepdims=True)
        return carry

    lax.fori_loop(0, CB // 2, turn, 0, unroll=4)


def _turns(cnt):
    return (cnt + GROUP - 1) // GROUP


def _group(ids, cnt, first, size):
    out = []
    for k in range(size):
        slot = first + k
        code = ids[0, slot]
        out.append((slot, code >> 5, code & (CB - 1), slot < cnt))
    return out


def fetch_kernel(users, out, sem):
    copy = pltpu.make_async_copy(users, out, sem)
    copy.start()
    copy.wait()


def first_kernel(count, users, part, peer, codes, kept0, kept1, keep, give, rows, lacc, racc, panel, scores, ids,
                 sems, fetched, stored):
    fetch = pltpu.make_async_copy(codes, ids, fetched)
    fetch.start()
    copies = [
        pltpu.make_async_copy(src.at[x], panel.at[:, x, half], sems.at[x, half])
        for x in range(NX)
        for half, src in enumerate((part, peer))
    ]
    for copy in copies:
        copy.start()
    _clear(lacc, racc)
    for copy in copies:
        copy.wait()
    fetch.wait()
    camps = panel.reshape(CB, BLOCK, E)
    cnt = count[0, 0]
    turns = _turns(cnt)
    kepts = (kept0, kept1)

    def products(g):
        return [
            lax.dot_general(
                camps[cb], users[ub], (((1,), (1,)), ((), ())), preferred_element_type=F32
            ).astype(jnp.bfloat16)
            for _, ub, cb, _ in _group(ids, cnt, g * GROUP, GROUP)
        ]

    def store(g, blocks):
        for k, block in enumerate(blocks):
            scores[g * GROUP + k] = block
        for which, kept in enumerate(kepts):
            _save(scores, kept, stored, which, g).start()

    def add(g):
        for slot, ub, cb, live in _group(ids, cnt, g * GROUP, GROUP):
            x = jnp.clip(scores[slot].astype(F32), 0.0, 1.0)
            lacc[jnp.where(live, cb, CB)] += x
            racc[jnp.where(live, ub, UB)] += _fold(x)

    store(0, products(0))

    def turn(g, carry):
        blocks = products(g)
        add(g - 1)
        store(g, blocks)
        return carry

    lax.fori_loop(1, turns, turn, 0)
    add(turns - 1)

    def finish(r, carry):
        pair = lacc[pl.ds(2 * r, 2)]
        for which, out in enumerate((keep, give)):
            both = pair[:, which * PART:(which + 1) * PART].reshape(BLOCK, BLOCK)
            out[pl.ds(r, 1), :] = jnp.sum(both.T, axis=0, keepdims=True)
        return carry

    lax.fori_loop(0, CB // 2, finish, 0, unroll=2)
    rows[...] = racc[:UB].sum(axis=1)
    for which, kept in enumerate(kepts):
        _each(turns, lambda g, w=which, k=kept: _save(scores, k, stored, w, g).wait())


def _duals(load_in, r0, r1, r2, r3, cap_i, lim_i, lam_in, mu_in):
    load = load_in[...]
    rows = (r0[...] + r2[...]) + (r1[...] + r3[...])
    cap = cap_i[...].astype(F32)
    lim = lim_i[...].astype(F32)
    lam_new = jnp.maximum(0.0, lam_in + (load - cap) / cap)
    mu_new = jnp.maximum(0.0, mu_in + (rows - lim) / lim)
    return load, cap, lim, lam_new, mu_new


def _round_kernel(id0, id1, count0, count1, load_in, r0, r1, r2, r3, cap_i, lim_i, lam_in, mu_in, kepts,
                  load, rows, values, lam_out, mu_out, lacc, racc, vacc, lamb, mub, scores, loaded):
    lists = ((id0, count0[0, 0]), (id1, count1[0, 0]))
    _each(_turns(lists[0][1]), lambda g: _load(kepts[0], scores, loaded, 0, g).start())
    _clear(lacc, racc, vacc)
    lam = 0.0 if lam_in is None else lam_in[...]
    mu = 0.0 if mu_in is None else mu_in[...]
    _, _, _, lam_new, mu_new = _duals(load_in, r0, r1, r2, r3, cap_i, lim_i, lam, mu)
    lam_out[...] = lam_new
    mu_out[...] = mu_new
    lam_bar = 2.0 * lam_new - lam
    mub[:UB2] = (2.0 * mu_new - mu)[:, None, :]
    for r in range(CB // 2):
        tall = jnp.broadcast_to(lam_bar[r:r + 1, :], (BLOCK, BLOCK)).T
        lamb[2 * r] = tall[:PART]
        lamb[2 * r + 1] = tall[PART:]
    _each(_turns(lists[1][1]), lambda g: _load(kepts[1], scores, loaded, 1, g).start())

    for which, (ids, cnt) in enumerate(lists):

        def some(first, ids=ids, cnt=cnt, which=which):
            for slot, ub, cb, live in _group(ids, cnt, first, STEP):
                s = scores[which * SLOTS + slot].astype(F32)
                x = jnp.clip(s - lamb[cb] - mub[ub + which * UB], 0.0, 1.0)
                lacc[jnp.where(live, cb, CB)] += x
                to_u = jnp.where(live, ub + which * UB, UB2)
                racc[to_u] += _fold(x)
                if vacc is not None:
                    vacc[to_u] += _fold(x * s)

        def chunk(g, which=which, some=some):
            _load(kepts[which], scores, loaded, which, g).wait()
            _each(GROUP // STEP, lambda i: some(g * GROUP + i * STEP))

        _each(_turns(cnt), chunk)

    _finish_load(lacc, load)
    rows[...] = racc[:UB2].sum(axis=1)
    if vacc is not None:
        values[...] = vacc[:UB2].sum(axis=1)


def second_kernel(id0, id1, count0, count1, load_in, r0, r1, r2, r3, cap_i, lim_i, kept0, kept1,
                  load, rows, lam_out, mu_out, lacc, racc, lamb, mub, scores, loaded):
    _round_kernel(id0, id1, count0, count1, load_in, r0, r1, r2, r3, cap_i, lim_i, None, None, (kept0, kept1),
                  load, rows, None, lam_out, mu_out, lacc, racc, None, lamb, mub, scores, loaded)


def third_kernel(id0, id1, count0, count1, load_in, r0, r1, r2, r3, cap_i, lim_i, lam_in, mu_in, kept0, kept1,
                 load, out, lam_out, mu_out, lacc, racc, vacc, lamb, mub, scores, loaded):
    _round_kernel(id0, id1, count0, count1, load_in, r0, r1, r2, r3, cap_i, lim_i, lam_in, mu_in, (kept0, kept1),
                  load, out.at[0], out.at[1], lam_out, mu_out, lacc, racc, vacc, lamb, mub, scores, loaded)


def last_kernel(core, p0, p1, p2, p3, lim_i, mu_in, mine, theirs, duals, user_duals, ratio, user_value):
    half = pl.ds(0, UB)
    rows, value = ((p0[k, half] + p2[k, half]) + (p1[k, half] + p3[k, half]) for k in range(2))
    lim = lim_i[half].astype(F32)
    user_duals[...] = jnp.maximum(0.0, mu_in[half] + (rows - lim) / lim)
    user_value[...] = value / lim
    first = core[0] == 0
    for k, out in enumerate((duals, ratio)):
        a, b = jnp.where(first, mine[k], theirs[k]), jnp.where(first, theirs[k], mine[k])
        even = jnp.concatenate([a[:, :PART], b[:, :PART]], axis=1)
        odd = jnp.concatenate([a[:, PART:], b[:, PART:]], axis=1)
        for r in range(CB // 2):
            out[2 * r:2 * r + 1, :] = even[r:r + 1]
            out[2 * r + 1:2 * r + 2, :] = odd[r:r + 1]


def campaigns_kernel(parts, cap_i, lam_in, out):
    load = parts[...].sum(0)
    cap = cap_i[...].astype(F32)
    out[0] = jnp.maximum(0.0, lam_in[...] + (load - cap) / cap)
    out[1] = load / cap


def spread_kernel(load, out):
    out[...] = jnp.broadcast_to(load[...][None], out.shape)


def spread_sum_kernel(keep, got, out):
    out[...] = jnp.broadcast_to((keep[...] + got[...])[None], out.shape)


def join_kernel(mine, theirs, out):
    out[:UB] = mine[...]
    out[UB:] = theirs[...]


def sum_kernel(parts, out):
    out[...] = parts[...].sum(0)


def pair_kernel(mine, theirs, out):
    half = pl.ds(0, UB)
    rest = pl.ds(UB, UB)
    out[..., half, :] = mine[..., half, :] + theirs[..., rest, :]
    out[..., rest, :] = mine[..., rest, :] + theirs[..., half, :]


SMEM = pl.BlockSpec(memory_space=pltpu.SMEM)
VMEM = pl.BlockSpec(memory_space=pltpu.VMEM)
ANY = pl.BlockSpec(memory_space=pl.ANY)


def _call(kernel, n_smem, args, outs, scratch=(), more=(), any_in=0, any_out=0, limit=4):
    return pl.pallas_call(
        kernel,
        in_specs=[SMEM] * n_smem + [VMEM] * (len(args) - n_smem - any_in) + [ANY] * any_in,
        out_specs=[ANY] * any_out + [VMEM] * (len(outs) - any_out),
        out_shape=[jax.ShapeDtypeStruct(s, d) for s, d in outs],
        scratch_shapes=[pltpu.VMEM(s, F32) for s in scratch] + list(more),
        compiler_params=pltpu.CompilerParams(vmem_limit_bytes=limit * 2 ** 20),
    )(*args)


LACC = (CB + 1, PART, BLOCK)
LACC1 = (CB + 1, BLOCK, BLOCK)
RACC1 = (UB + 1, 8, BLOCK)
RACC = (UB2 + 1, 8, BLOCK)
LOAD = ((CB // 2, BLOCK), F32)
ROWS = ((UB2, BLOCK), F32)
MUB = (UB2, 1, BLOCK)
LAMB = (CB, PART, BLOCK)
SCORES = ((SLOTS, PART, BLOCK), jnp.bfloat16)
ROOMY = ((2 * SLOTS, PART, BLOCK), jnp.bfloat16)
KEPT = [pltpu.VMEM((2 * SLOTS, PART, BLOCK), jnp.bfloat16), pltpu.SemaphoreType.DMA((2 * CHUNKS,))]


def _spread(x, axes, n):
    return lax.all_to_all(jnp.broadcast_to(x[None], (n,) + x.shape), axes, 0, 0, tiled=True)


def _swap(x):
    return lax.ppermute(x, "core", [(0, 1), (1, 0)])


def _load_parts(load):
    (wide,) = _call(spread_kernel, 0, (load,), [((NZ * NX,) + LOAD[0], F32)])
    return lax.all_to_all(wide, ("z", "x"), 0, 0, tiled=True)


def _shift(x, k):
    return lax.ppermute(x, "camp", [((i + k) % NCAMP, i) for i in range(NCAMP)])


def _camp_parts(x, kernel, shape):
    (x,) = _call(kernel, 0, (x, _swap(x)), [(shape, F32)])
    return x, _shift(x, 1), _shift(x, 2), _shift(x, 3)


def shards(user_emb, camp_emb, block_ids, block_count, capacity, user_limit):
    where = jnp.reshape(lax.axis_index("core"), (1,)).astype(jnp.int32)
    camp_emb, where = lax.optimization_barrier((camp_emb, where))
    users = user_emb.reshape(UB, BLOCK, E)

    part = _spread(camp_emb, "z", NZ)
    part = _spread(part.reshape(NZ, PART, E), "x", NX).reshape(NX, NZ, PART, E)
    part, users = lax.optimization_barrier((part, users))
    (users,) = _call(
        fetch_kernel, 0, (users,), [(users.shape, users.dtype)], [], [pltpu.SemaphoreType.DMA], any_in=1)
    peer = _swap(part)

    kept0, give1, keep, give, rows = _call(
        first_kernel, 1, (block_count, users, part, peer, block_ids), [ROOMY, SCORES, LOAD, LOAD, ((UB, BLOCK), F32)],
        [LACC1, RACC1],
        [pltpu.VMEM((NZ, NX, 2, PART, E), jnp.bfloat16), pltpu.VMEM((SLOTS, BLOCK, BLOCK), jnp.bfloat16),
         pltpu.SMEM((1, SLOTS), jnp.int32), pltpu.SemaphoreType.DMA((NX, 2)), pltpu.SemaphoreType.DMA,
         pltpu.SemaphoreType.DMA((2, CHUNKS))], any_in=1, any_out=2, limit=FIRST)
    (wide,) = _call(spread_sum_kernel, 0, (keep, _swap(give)), [((NZ * NX,) + LOAD[0], F32)])
    wide, rows, give1, block_ids, block_count, user_limit, capacity = lax.optimization_barrier(
        (wide, rows, give1, block_ids, block_count, user_limit, capacity))
    wide = lax.all_to_all(wide, ("z", "x"), 0, 0, tiled=True)
    parts = _camp_parts(rows, join_kernel, ROWS[0])
    kept1 = _swap(give1)
    ids1, count1, lim1 = _swap(block_ids), _swap(block_count), _swap(user_limit)
    halves = capacity.reshape(CB // 2, 2, 2, PART)
    cap = jnp.where(where[0] == 0, halves[:, :, 0], halves[:, :, 1]).reshape(CB // 2, BLOCK)
    lim = jnp.concatenate([user_limit, lim1]).reshape(UB2, BLOCK)
    lists = (block_ids, ids1, block_count, count1)
    (load,) = _call(sum_kernel, 0, (wide,), [LOAD])

    load, rows, lam, mu = _call(
        second_kernel, 4, (*lists, load, *parts, cap, lim, kept0, kept1),
        [LOAD, ROWS, LOAD, ROWS], [LACC, RACC, LAMB, MUB], KEPT, any_in=2, limit=WIDE)
    parts = _camp_parts(rows, pair_kernel, ROWS[0])
    (load,) = _call(sum_kernel, 0, (_load_parts(load),), [LOAD])
    load, sums, lam, mu = _call(
        third_kernel, 4, (*lists, load, *parts, cap, lim, lam, mu, kept0, kept1),
        [LOAD, ((2, UB2, BLOCK), F32), LOAD, ROWS], [LACC, RACC, RACC, LAMB, MUB], KEPT, any_in=2, limit=WIDE)
    parts = _camp_parts(sums, pair_kernel, (2,) + ROWS[0])
    (pair,) = _call(campaigns_kernel, 0, (_load_parts(load), cap, lam), [((2, CB // 2, BLOCK), F32)])
    duals, user_duals, ratio, value = _call(
        last_kernel, 1, (where, *parts, lim, mu, pair, _swap(pair)),
        [((CB, BLOCK), F32), ((UB, BLOCK), F32)] * 2)
    return duals.reshape(-1), user_duals.reshape(-1), ratio.reshape(-1), value.reshape(-1)


def solution(mesh):
    fine = Mesh(mesh.devices.reshape(NZ, NX, NCORE, NCAMP), ("z", "x", "core", "camp"))
    users = ("z", "x", "core")
    return jax.shard_map(
        shards,
        mesh=fine,
        in_specs=(P(users, None), P(("camp",) + users, None), P("camp", users), P("camp", users), P("camp"), P(users)),
        out_specs=(P("camp"), P(users), P("camp"), P(users)),
        check_vma=False,
    )
```
